256 devices in a mesh: fine: 32 (over x, z), coarse: 8 (over y, core).
Axes of the slice: x: 4, y: 4, z: 8, core: 2. Of those that a mesh axis runs over, the one named last changes fastest.
Arguments:
- fine_blocks: float32 [7, 10, 10, 131072], P(None, None, None, ('fine', 'coarse')), may hold values from -0.035 to 0.835
- fine_columns: int32 [7, 131072], P(None, ('fine', 'coarse')), may hold values from 0 to 1279, as said below
- coarse_slots: int32 [7, 131072], P(None, ('fine', 'coarse')), may hold values from 0 to 6, as said below
- ghost_lists: int32 [196608], P(('fine', 'coarse')), may hold values from 0 to 511, as said below
- tentative: float32 [10, 10, 131072], P(None, None, ('fine', 'coarse')), may hold values from -0.05 to 1.05
- members: int32 [15, 16384], P(None, ('fine', 'coarse')), may hold values from -1 to 511, as said below
- coarse_columns: int32 [7, 16384], P(None, ('fine', 'coarse')), may hold values from 0 to 191, as said below
- coarse_rhs: float32 [10, 16384], P(None, ('fine', 'coarse')), may hold values from -6 to 6
- coarse_guess: float32 [10, 16384], P(None, ('fine', 'coarse')), may hold values from -6 to 6
Outputs:
- coarse_op: float32 [7, 10, 10, 16384], P(None, None, None, ('fine', 'coarse'))
- coarse_iterate: float32 [10, 16384], P(None, ('fine', 'coarse'))
The draws below stay inside these ranges and needn't reach their ends.
Inputs may be any that keep to these rules, and one draw needn't show every extreme that they name: `fine_columns`: in block g, values below 512 are the block's own cells, 512 + p is the p-th listed cell of block g-1 and 896 + p the p-th listed cell of block g+1; row 0 names the cell itself; the first block never reads block g-1 and the last never block g+1; the cell named lies in the aggregate that coarse_columns names for the coarse block of coarse_slots. `coarse_slots`: row 0 is 0 and every other row lies in 1 to 6. `ghost_lists`: each half of a block's 384 * 2 values lists distinct cells of the neighbouring block, local to it. `members`: the lists of a block's aggregates hold each of its cells exactly once, filled from the top and padded with -1; every block has an aggregate of 15 cells and one of 1 cell. `coarse_columns`: row 0 names the row's own aggregate and no other row does; the first block names no aggregate of block g-1, the last none of block g+1.
All inputs are finite; a program needn't handle non-finite values.
Results may differ from the reference program's by a relative error of at most 0.0003.
Values sent between devices are 32-bit elements; how exact they have to be, the bound alone decides.
A program may use at most 64 MiB of HBM per device.

```python
import jax
import jax.numpy as jnp
from jax import lax

B = 10
K = 7
KC = 7
AVG = 8
SWEEPS = 2
C_DEV = 512
LIST = 15
H = 384
NA_DEV = 64
NDEV = 256
NCELL = 131072
NAGG = 16384


def read_list(list_key):
    order = jax.random.permutation(list_key, C_DEV).astype(jnp.int32)
    where_last = jnp.argmax(order == C_DEV - 1)
    order = order.at[where_last].set(order[0]).at[0].set(C_DEV - 1)
    return order[:H].astype(jnp.int32)


def block_tables(dev_key):
    key_sizes, key_perm, key_order, key_prev, key_next = jax.random.split(dev_key, 5)
    half_count = NA_DEV // 2
    spread = jax.random.randint(key_sizes, (half_count,), -(AVG - 1), AVG)
    spread = spread.at[0].set(AVG - 1)
    agg_sizes = jnp.concatenate([AVG + spread, AVG - spread])
    agg_sizes = agg_sizes[jax.random.permutation(key_perm, NA_DEV)].astype(jnp.int32)
    shuffle = jax.random.permutation(key_order, C_DEV).astype(jnp.int32)
    agg_ends = jnp.cumsum(agg_sizes).astype(jnp.int32)
    starts = agg_ends - agg_sizes
    list_place = jnp.arange(LIST, dtype=jnp.int32)[:, None]
    position = jnp.minimum(starts[None, :] + list_place, C_DEV - 1)
    member_table = jnp.where(list_place < agg_sizes[None, :], shuffle[position], -1).astype(jnp.int32)
    cell_place = jnp.arange(C_DEV, dtype=jnp.int32)
    owner_of_pos = jnp.searchsorted(agg_ends, cell_place, side='right').astype(jnp.int32)
    cell_agg = jnp.zeros((C_DEV,), jnp.int32).at[shuffle].set(owner_of_pos)
    member_rank = jnp.zeros((C_DEV,), jnp.int32).at[shuffle].set(cell_place - starts[owner_of_pos])
    read_prev = read_list(key_prev)
    read_next = read_list(key_next)
    return (agg_sizes, member_table, cell_agg, member_rank, read_prev, read_next)


def list_inverse(read_list_values):
    return jnp.full((C_DEV,), H, jnp.int32).at[read_list_values].set(jnp.arange(H, dtype=jnp.int32))


def layout_tables(key):
    device_keys = jax.random.split(key, NDEV)
    agg_sizes, member_table, cell_agg, member_rank, read_prev, read_next = jax.vmap(block_tables)(device_keys)
    inv_prev = jax.vmap(list_inverse)(read_prev)
    inv_next = jax.vmap(list_inverse)(read_next)
    entry_keys = jax.random.split(jax.random.fold_in(key, 7), NDEV)

    def entries(entry_key, device):
        key_other, key_ghost, key_slot, key_first, key_member = jax.random.split(entry_key, 5)
        earlier = jnp.maximum(device - 1, 0)
        later = jnp.minimum(device + 1, NDEV - 1)
        agg_ids = jnp.arange(NA_DEV, dtype=jnp.int32)[None, :]
        slot_ids = jnp.arange(KC, dtype=jnp.int32)[:, None]
        other_agg = (agg_ids + 1 + jax.random.randint(key_other, (KC, NA_DEV), 0, NA_DEV - 1)) % NA_DEV
        ghost_pos = jax.random.randint(key_ghost, (KC, NA_DEV), 0, H)
        prev_agg = cell_agg[earlier][read_prev[device][ghost_pos]]
        next_agg = cell_agg[later][read_next[device][ghost_pos]]
        slot_kind = jnp.where((slot_ids >= 3) & (slot_ids <= 4) & (device > 0), 1, jnp.where((slot_ids >= 5) & (device < NDEV - 1), 2, 0))
        coarse_cols = jnp.where(slot_ids == 0, NA_DEV + agg_ids, jnp.where(slot_kind == 1, prev_agg, jnp.where(slot_kind == 2, 2 * NA_DEV + next_agg, NA_DEV + other_agg))).astype(jnp.int32)
        random_slot = jax.random.randint(key_slot, (K - 1, C_DEV), 1, KC)
        scores = jax.random.randint(key_first, (K - 1, C_DEV), 0, 1 << 30)
        first_slots = jnp.argsort(scores, axis=0, stable=True).astype(jnp.int32) + 1
        chosen = jnp.where(member_rank[device][None, :] == 0, first_slots, random_slot).astype(jnp.int32)
        own_agg = cell_agg[device][None, :]
        target = coarse_cols[chosen, own_agg]
        entry_kind = slot_kind[:, 0][chosen]
        fallback = ghost_pos[chosen, own_agg]
        member_draw = jax.random.randint(key_member, (K - 1, C_DEV), 0, 1 << 20)

        def member_of(table_index, local_agg):
            sizes_here = agg_sizes[table_index][local_agg]
            return member_table[table_index][member_draw % sizes_here, local_agg]
        own_cell = member_of(device, jnp.clip(target - NA_DEV, 0, NA_DEV - 1))
        prev_cell = member_of(earlier, jnp.clip(target, 0, NA_DEV - 1))
        next_cell = member_of(later, jnp.clip(target - 2 * NA_DEV, 0, NA_DEV - 1))
        prev_spot = inv_prev[device][prev_cell]
        prev_spot = jnp.where(prev_spot < H, prev_spot, fallback)
        next_spot = inv_next[device][next_cell]
        next_spot = jnp.where(next_spot < H, next_spot, fallback)
        rest = jnp.where(entry_kind == 1, C_DEV + prev_spot, jnp.where(entry_kind == 2, C_DEV + H + next_spot, own_cell))
        fine_cols = jnp.concatenate([jnp.arange(C_DEV, dtype=jnp.int32)[None, :], rest.astype(jnp.int32)], axis=0)
        fine_slots = jnp.concatenate([jnp.zeros((1, C_DEV), jnp.int32), chosen], axis=0)
        return (coarse_cols, fine_cols, fine_slots)
    coarse_cols, fine_cols, fine_slots = jax.vmap(entries)(entry_keys, jnp.arange(NDEV, dtype=jnp.int32))
    ghost_table = jnp.concatenate([read_prev, read_next], axis=1)
    return (member_table, ghost_table, coarse_cols, fine_cols, fine_slots)


def draw_fine_columns(key, part):
    tables = layout_tables(key)
    return jnp.transpose(tables[3], (1, 0, 2)).reshape(K, NCELL).astype(jnp.int32)


def draw_coarse_slots(key, part):
    tables = layout_tables(key)
    return jnp.transpose(tables[4], (1, 0, 2)).reshape(K, NCELL).astype(jnp.int32)


def draw_ghost_lists(key, part):
    tables = layout_tables(key)
    return tables[1].reshape(2 * H * NDEV).astype(jnp.int32)


def draw_members(key, part):
    tables = layout_tables(key)
    return jnp.transpose(tables[0], (1, 0, 2)).reshape(LIST, NAGG).astype(jnp.int32)


def draw_coarse_columns(key, part):
    tables = layout_tables(key)
    return jnp.transpose(tables[2], (1, 0, 2)).reshape(KC, NAGG).astype(jnp.int32)


def draw_fine_blocks(key, part):
    key = jax.random.fold_in(key, 11)
    key_diag, key_near, key_far = jax.random.split(key, 3)
    diagonal = jax.random.uniform(key_diag, (B, NCELL), jnp.float32, 0.4, 0.8)
    near = jax.random.uniform(key_near, (B, B, NCELL), jnp.float32, -0.035, 0.035)
    far = jax.random.uniform(key_far, (K - 1, B, B, NCELL), jnp.float32, -0.02, 0.02)
    identity = jnp.eye(B, dtype=jnp.float32)[:, :, None]
    first = identity * diagonal[:, None, :] + near
    return jnp.concatenate([first[None], far], axis=0).astype(jnp.float32)


def draw_tentative(key, part):
    key = jax.random.fold_in(key, 13)
    noise = jax.random.uniform(key, (B, B, NCELL), jnp.float32, -0.05, 0.05)
    identity = jnp.eye(B, dtype=jnp.float32)[:, :, None]
    return (identity + noise).astype(jnp.float32)


def level_of(own_key, shape, cuts, smallest, largest):
    loudness = 1.0
    for axis_at, blocks in cuts:
        heights = jax.random.uniform(jax.random.fold_in(jax.random.fold_in(own_key, 6), axis_at), (blocks,), jnp.float32, smallest / len(cuts), largest / len(cuts))
        loudness = loudness * jnp.repeat(jnp.exp(heights), shape[axis_at] // blocks).reshape((-1,) + (1,) * (len(shape) - 1 - axis_at))
    return loudness


def bell_draw(stream_key, shape, width, reach, cuts=(), held_as=jnp.bfloat16):
    drawn = jax.random.normal(stream_key, shape, jnp.float32) * width
    if len(cuts) > 0:
        drawn = level_of(stream_key, shape, cuts, -0.22, 0.18) * drawn
    return jnp.clip(drawn, min=-reach, max=reach).astype(held_as)


def setup_inputs(seed: int = 0) -> dict:
    arg_keys = jax.random.split(jax.random.key(seed), 10)
    return {
        "fine_blocks": draw_fine_blocks(jax.random.fold_in(arg_keys[9], 71), 0),
        "fine_columns": draw_fine_columns(jax.random.fold_in(arg_keys[9], 71), 0),
        "coarse_slots": draw_coarse_slots(jax.random.fold_in(arg_keys[9], 71), 0),
        "ghost_lists": draw_ghost_lists(jax.random.fold_in(arg_keys[9], 71), 0),
        "tentative": draw_tentative(jax.random.fold_in(arg_keys[9], 71), 0),
        "members": draw_members(jax.random.fold_in(arg_keys[9], 71), 0),
        "coarse_columns": draw_coarse_columns(jax.random.fold_in(arg_keys[9], 71), 0),
        "coarse_rhs": bell_draw(arg_keys[7], (B, NAGG), 1.0, 6.0, ((1, 256),), jnp.float32),
        "coarse_guess": bell_draw(arg_keys[8], (B, NAGG), 1.0, 6.0, ((1, 256),), jnp.float32),
    }


def reference(fine_blocks, fine_columns, coarse_slots, ghost_lists, tentative, members, coarse_columns, coarse_rhs, coarse_guess):
    highest = lax.Precision.HIGHEST
    zero_rim = jnp.zeros((B, B, C_DEV), tentative.dtype)
    padded = jnp.concatenate([zero_rim, tentative, zero_rim], axis=2)
    slot_range = jnp.arange(KC, dtype=jnp.int32)

    def one_block(device):
        start = device * C_DEV
        own_blocks = lax.dynamic_slice_in_dim(fine_blocks, start, C_DEV, 3)
        own_cols = lax.dynamic_slice_in_dim(fine_columns, start, C_DEV, 1)
        own_slots = lax.dynamic_slice_in_dim(coarse_slots, start, C_DEV, 1)
        lists = lax.dynamic_slice_in_dim(ghost_lists, device * (2 * H), 2 * H, 0)
        before = lax.dynamic_slice_in_dim(padded, start, C_DEV, 2)
        own_basis = lax.dynamic_slice_in_dim(padded, start + C_DEV, C_DEV, 2)
        after = lax.dynamic_slice_in_dim(padded, start + 2 * C_DEV, C_DEV, 2)
        extended = jnp.concatenate([own_basis, before[:, :, lists[:H]], after[:, :, lists[H:]]], axis=2)
        picked_basis = extended[:, :, own_cols]
        ap_blocks = jnp.einsum('kijc,jlkc->kilc', own_blocks, picked_basis, precision=highest)
        product = jnp.einsum('jic,kjlc->kilc', own_basis, ap_blocks, precision=highest)
        onehot = (own_slots[:, None, :] == slot_range[None, :, None]).astype(product.dtype)
        per_slot = jnp.einsum('kilc,ksc->silc', product, onehot, precision=highest)
        own_members = lax.dynamic_slice_in_dim(members, device * NA_DEV, NA_DEV, 1)
        weight = (own_members >= 0).astype(per_slot.dtype)
        gathered = per_slot[:, :, :, jnp.maximum(own_members, 0)]
        return jnp.sum(gathered * weight, axis=3)
    pieces = lax.map(one_block, jnp.arange(NDEV, dtype=jnp.int32))
    coarse_op = jnp.moveaxis(pieces, 0, 3).reshape(KC, B, B, NAGG)
    agg_index = jnp.arange(NAGG, dtype=jnp.int32)
    global_cols = (agg_index // NA_DEV)[None, :] * NA_DEV + coarse_columns - NA_DEV
    global_cols = jnp.clip(global_cols, 0, NAGG - 1).astype(jnp.int32)
    diagonal = jnp.transpose(coarse_op[0], (2, 0, 1))
    iterate = coarse_guess
    for sweep in range(SWEEPS):
        neighbours = iterate[:, global_cols]
        applied = jnp.einsum('sijn,jsn->in', coarse_op, neighbours, precision=highest)
        residual = coarse_rhs - applied
        update = jnp.linalg.solve(diagonal, jnp.transpose(residual)[:, :, None])[:, :, 0]
        iterate = iterate + jnp.transpose(update)
    return (coarse_op, iterate)
```

```python
import functools

import jax
import jax.numpy as jnp
from jax import lax
from jax.experimental import pallas as pl
from jax.experimental.pallas import tpu as pltpu
from jax.sharding import PartitionSpec as P

F32 = jnp.float32
BF16 = jnp.bfloat16
MESH = pl.DeviceIdType.MESH
LANES = 128


def lane_gather(table, index):
    return jnp.take_along_axis(table, index, axis=1, mode="promise_in_bounds")


def halves(value):
    high = value.astype(BF16)
    low = (value - high.astype(F32)).astype(BF16)
    return high, low


def dot_nn(left, right):
    return lax.dot_general(left, right, (((1,), (0,)), ((), ())), preferred_element_type=F32)


def dot_nt(left, right):
    return lax.dot_general(left, right, (((1,), (1,)), ((), ())), preferred_element_type=F32)


def kernel(
    n_fine, n_coarse,
    a_hbm, col_hbm, slot_hbm, ghost_hbm, p_hbm, mem_hbm, cc_hbm, rhs_hbm, guess_hbm,
    op_ref, it_ref,
    a_v, col_v, slot_v, ghost_v, p_v, mem_v, cc_v, rhs_v, guess_v,
    v_pad, rhs_pad, v_one, v_near, v_far,
    mt_s, m_s, w_own, w_near, w_far, pc_own, pc_near, pc_far,
    q_s, d_s, inv_s, idx_s, cc_s, oh_own, oh_near, oh_far,
    phl_s, whl_s, wacc_s, wg_s, acc_s, g_s, prod_s, z_s, lhs_s, rt_s, op_s,
    in_sem, send_sem, recv_sem,
):
    n_all = n_fine * n_coarse
    me = lax.axis_index("fine") * n_coarse + lax.axis_index("coarse")
    odd = lax.rem(me, 2)
    near = me + 1 - 2 * odd
    far = lax.rem(me + n_all - 1 + 2 * odd, n_all)
    near_id = (near // n_coarse, lax.rem(near, n_coarse))
    far_id = (far // n_coarse, lax.rem(far, n_coarse))

    barrier = pltpu.get_barrier_semaphore()
    pl.semaphore_signal(barrier, inc=1, device_id=far_id, device_id_type=MESH)
    pl.semaphore_signal(barrier, inc=1, device_id=near_id, device_id_type=MESH)

    order, agg_count = rhs_v.shape
    fine_rows = a_v.shape[2]
    slots = cc_v.shape[0]
    cells = p_v.shape[2]
    tiles = cells // LANES
    rows = pc_own.shape[0]
    span = rows * 8
    rest = fine_rows - 1

    pairs = [(p_hbm, p_v), (mem_hbm, mem_v), (guess_hbm, guess_v), (col_hbm, col_v), (ghost_hbm, ghost_v),
             (slot_hbm, slot_v), (cc_hbm, cc_v), (rhs_hbm, rhs_v), (a_hbm, a_v)]
    loads = [pltpu.make_async_copy(src, dst, in_sem.at[i]) for i, (src, dst) in enumerate(pairs)]
    for load in loads:
        load.start()

    loads[1].wait()
    cell_row = lax.broadcasted_iota(jnp.int32, (cells, agg_count), 0)
    found = None
    for place in range(mem_v.shape[0]):
        hit = cell_row == mem_v[place:place + 1, :]
        found = hit if found is None else jnp.logical_or(found, hit)
    mt_s[...] = jnp.where(found, 1.0, 0.0).astype(BF16)
    eye = jnp.where(
        lax.broadcasted_iota(jnp.int32, (agg_count, agg_count), 0)
        == lax.broadcasted_iota(jnp.int32, (agg_count, agg_count), 1), 1.0, 0.0).astype(BF16)
    m_s[...] = dot_nt(eye, mt_s[...]).astype(BF16)

    loads[2].wait()
    v_pad[...] = jnp.zeros_like(v_pad)
    v_pad[0:order, :] = guess_v[...]
    high, low = halves(v_pad[...])
    v_cells = (dot_nn(high, m_s[...]) + dot_nn(low, m_s[...]))[0:order, :]
    loads[0].wait()
    w_own[...] = jnp.zeros_like(w_own)
    for j in range(order):
        w_own[j:j + 1, :] = jnp.sum(p_v[j] * v_cells, axis=0, keepdims=True)
    pc_own[...] = jnp.zeros_like(pc_own)
    for j in range(order):
        pc_own[order * j:order * (j + 1), :] = p_v[j]

    pl.semaphore_wait(barrier, 2)

    def send(source, to_near, to_far, base):
        made = []
        for at, (dst, ident) in enumerate(((to_far, far_id), (to_near, near_id))):
            copy = pltpu.make_async_remote_copy(
                src_ref=source, dst_ref=dst, send_sem=send_sem.at[base + at], recv_sem=recv_sem.at[base + at],
                device_id=ident, device_id_type=MESH)
            copy.start()
            made.append(copy)
        return made

    w_sent = send(w_own, w_near, w_far, 0)
    p_sent = send(pc_own, pc_near, pc_far, 2)

    loads[8].wait()

    def q_step(step, carry):
        pair = step // tiles
        lanes = pl.ds(pl.multiple_of(lax.rem(step, tiles) * LANES, LANES), LANES)
        blocks = [[a_v[r, pair * 2 + jj, :, lanes] for r in range(order)] for jj in range(2)]
        for i in range(order):
            total = [None, None]
            for r in range(order):
                basis = p_v[r, i:i + 1, lanes]
                for jj in range(2):
                    term = basis * blocks[jj][r]
                    total[jj] = term if total[jj] is None else total[jj] + term
            for jj in range(2):
                q_s[i, pair * 2 + jj, :, lanes] = total[jj]
        return carry

    lax.fori_loop(0, order // 2 * tiles, q_step, 0)

    d_s[...] = jnp.zeros_like(d_s)

    def d_step(i, carry):
        total = None
        for j in range(order):
            term = q_s[i, j, 0:1, :] * p_v[j]
            total = term if total is None else total + term
        d_s[i, 0:order, :] = total
        return carry

    lax.fori_loop(0, order, d_step, 0)
    deep = d_s.shape[1]
    high, low = halves(d_s[...].reshape(order * deep, cells))
    diagonal = (dot_nt(high, m_s[...]) + dot_nt(low, m_s[...])).reshape(order, deep, agg_count)
    wide = jnp.zeros((order, LANES - agg_count), F32)
    for i in range(order):
        op_s[pl.ds(i * order * 8, order, stride=8), :] = jnp.concatenate([diagonal[i, 0:order, :], wide], axis=1)
    inverse = diagonal
    entry = lax.broadcasted_iota(jnp.int32, (deep, agg_count), 0)
    row_at = lax.broadcasted_iota(jnp.int32, (order, 1, agg_count), 0)
    for pivot in range(order):
        line = inverse[pivot]
        scale = 1.0 / line[pivot:pivot + 1, :]
        line = jnp.where(entry == pivot, 1.0, line) * scale
        factor = inverse[:, pivot:pivot + 1, :]
        kept = jnp.where((entry == pivot)[None], 0.0, inverse)
        inverse = kept - factor * line[None]
        inverse = jnp.where(row_at == pivot, line[None], inverse)
    inv_s[...] = inverse

    loads[3].wait()
    loads[4].wait()
    idx_s[...] = jnp.zeros_like(idx_s)
    idx_s[0, 0:fine_rows, :] = col_v[...]
    is_odd = jnp.full((8, LANES), odd, jnp.int32)
    half = ghost_v.shape[0] * LANES // 2
    for t in range(tiles):
        at = slice(t * LANES, (t + 1) * LANES)
        col = idx_s[0, :, at]
        place = jnp.maximum(col - cells, 0)
        lane = jnp.bitwise_and(place, LANES - 1)
        part = jnp.right_shift(place, 7)
        cell = jnp.zeros((8, LANES), jnp.int32)
        for b in range(ghost_v.shape[0]):
            got = lane_gather(jnp.broadcast_to(ghost_v[b:b + 1, :], (8, LANES)), lane)
            cell = jnp.where(part == b, got, cell)
        own = col < cells
        after = jnp.where(col >= cells + half, 1, 0)
        same = after != is_odd
        idx_s[1, :, at] = jnp.where(own, col, -1)
        idx_s[2, :, at] = jnp.where(jnp.logical_and(jnp.logical_not(own), same), cell, -1)
        idx_s[3, :, at] = jnp.where(jnp.logical_or(own, same), -1, cell)
    ramp = lax.broadcasted_iota(jnp.int32, (256, cells), 0).astype(F32).astype(BF16)
    one = jnp.ones((256, cells), BF16)
    zero = jnp.zeros((256, cells), BF16)
    for group, hot in ((1, oh_own), (2, oh_near), (3, oh_far)):
        for k in range(rest):
            for block in range(cells // 256):
                line = (idx_s[group, k + 1:k + 2, :] - 256 * block).astype(F32).astype(BF16)
                hot[256 * block:256 * (block + 1), k * cells:(k + 1) * cells] = jnp.where(ramp == line, one, zero)

    loads[5].wait()
    member = m_s[...]
    none = jnp.zeros_like(member)
    for k in range(rest):
        line = slot_v[k + 1:k + 2, :].astype(F32).astype(BF16)
        wide_line = jnp.broadcast_to(line, (agg_count, cells))
        for s in range(1, slots):
            picked = wide_line == jnp.full((agg_count, cells), s, BF16)
            rt_s[(s - 1) * agg_count:s * agg_count, k * cells:(k + 1) * cells] = jnp.where(picked, member, none)

    def split_basis(source):
        high, low = halves(source[...])
        phl_s[0:rows, :] = high
        phl_s[rows:2 * rows, :] = low

    def basis_part(hot, k):
        both = dot_nn(phl_s[...], hot[:, k * cells:(k + 1) * cells])
        return both[0:rows, :] + both[rows:2 * rows, :]

    def vector_part(source, hot, k):
        both = dot_nn(whl_s[...], hot[:, k * cells:(k + 1) * cells])
        return both[0:16, :] + both[16:32, :]

    def split_vector(source):
        high, low = halves(source[...])
        whl_s[0:16, :] = high
        whl_s[16:32, :] = low

    split_basis(pc_own)
    split_vector(w_own)
    for k in range(rest):
        at = slice(k * cells, (k + 1) * cells)
        acc_s[:, at] = basis_part(oh_own, k)
        wacc_s[:, at] = vector_part(w_own, oh_own, k)
    w_sent[1].wait_recv()
    split_vector(w_near)
    for k in range(rest):
        at = slice(k * cells, (k + 1) * cells)
        wacc_s[:, at] += vector_part(w_near, oh_near, k)
    p_sent[1].wait_recv()
    split_basis(pc_near)
    for k in range(rest):
        at = slice(k * cells, (k + 1) * cells)
        acc_s[:, at] += basis_part(oh_near, k)

    loads[7].wait()
    rhs_pad[...] = jnp.zeros_like(rhs_pad)
    rhs_pad[0:order, :] = rhs_v[...]
    z_s[...] = jnp.zeros_like(z_s)
    for t in range(tiles):
        wg_s[pl.ds(t * LANES, 16, stride=8), :] = w_own[:, t * LANES:(t + 1) * LANES]
    w_sent[0].wait_recv()
    split_vector(w_far)
    for k in range(rest):
        total = wacc_s[:, k * cells:(k + 1) * cells] + vector_part(w_far, oh_far, k)
        for t in range(tiles):
            wg_s[pl.ds(t * LANES + k + 1, 16, stride=8), :] = total[:, t * LANES:(t + 1) * LANES]
    for t in range(tiles):
        at = slice(t * LANES, (t + 1) * LANES)
        taken = [wg_s[t * LANES + j * 8:t * LANES + j * 8 + fine_rows, :] for j in range(order)]
        for i in range(order):
            total = None
            for j in range(order):
                term = q_s[i, j, :, at] * taken[j]
                total = term if total is None else total + term
            z_s[i:i + 1, at] = jnp.sum(total, axis=0, keepdims=True)
    high, low = halves(z_s[...])
    applied = dot_nt(high, m_s[...]) + dot_nt(low, m_s[...])
    residual = rhs_pad[...] - applied
    v_one[...] = jnp.zeros_like(v_one)
    for i in range(order):
        update = jnp.sum(inv_s[i] * residual, axis=0, keepdims=True)
        v_one[i:i + 1, 0:agg_count] = v_pad[i:i + 1, :] + update
    v_sent = send(v_one, v_near, v_far, 4)

    p_sent[0].wait_recv()
    split_basis(pc_far)
    for k in range(rest):
        total = acc_s[:, k * cells:(k + 1) * cells] + basis_part(oh_far, k)
        for t in range(tiles):
            g_s[pl.ds(t * span + k + 1, rows, stride=8), :] = total[:, t * LANES:(t + 1) * LANES]

    def product_step(step, carry):
        pair = step // tiles
        t = lax.rem(step, tiles)
        lanes = pl.ds(pl.multiple_of(t * LANES, LANES), LANES)
        base = t * span + pair * 16
        taken = [[g_s[pl.ds(pl.multiple_of(base + (j * order + ll) * 8, 8), fine_rows), :] for j in range(order)]
                 for ll in range(2)]
        for i in range(order):
            total = [None, None]
            for j in range(order):
                left = q_s[i, j, :, lanes]
                for ll in range(2):
                    term = left * taken[ll][j]
                    total[ll] = term if total[ll] is None else total[ll] + term
            for ll in range(2):
                prod_s[pl.ds(pl.multiple_of(base + (i * order + ll) * 8, 8), fine_rows), :] = total[ll]
        return carry

    lax.fori_loop(0, order // 2 * tiles, product_step, 0)
    for k in range(rest):
        for t in range(tiles):
            high, low = halves(prod_s[pl.ds(t * span + k + 1, rows, stride=8), :])
            at = slice(k * cells + t * LANES, k * cells + (t + 1) * LANES)
            lhs_s[0:rows, at] = high
            lhs_s[rows:2 * rows, at] = low
    both = dot_nt(lhs_s[...], rt_s[...])
    summed = both[0:rows, :] + both[rows:2 * rows, :]
    filler = jnp.zeros((order * order, LANES - agg_count), F32)
    for s in range(1, slots):
        part = summed[0:order * order, (s - 1) * agg_count:s * agg_count]
        op_s[pl.ds(s, order * order, stride=8), :] = jnp.concatenate([part, filler], axis=1)
    for i in range(order):
        for l in range(order):
            op_ref[i, l] = op_s[(i * order + l) * 8:(i * order + l) * 8 + slots, 0:agg_count]

    loads[6].wait()
    cc_s[...] = jnp.zeros_like(cc_s)
    cc_s[0:slots, 0:agg_count] = cc_v[...]
    column = cc_s[...]
    lane = jnp.bitwise_and(column, agg_count - 1)
    holder = column // agg_count
    is_near = holder == 2 - 2 * is_odd
    is_far = holder == 2 * is_odd
    first = lane + jnp.where(is_near, agg_count, 0)
    v_sent[1].wait_recv()
    v_sent[0].wait_recv()
    nearby = jnp.concatenate([v_one[:, 0:agg_count], v_near[:, 0:agg_count]], axis=1)
    distant = v_far[...]
    names = []
    for l in range(order):
        one_side = lane_gather(jnp.broadcast_to(nearby[l:l + 1, :], (8, LANES)), first)
        other = lane_gather(jnp.broadcast_to(distant[l:l + 1, :], (8, LANES)), lane)
        names.append(jnp.where(is_far, other, one_side)[0:slots, 0:agg_count])
    lines = []
    z2 = rhs_pad
    for i in range(order):
        total = None
        for l in range(order):
            term = op_s[(i * order + l) * 8:(i * order + l) * 8 + slots, 0:agg_count] * names[l]
            total = term if total is None else total + term
        z2[i:i + 1, :] = rhs_v[i:i + 1, :] - jnp.sum(total, axis=0, keepdims=True)
    residual = z2[...]
    for i in range(order):
        update = jnp.sum(inv_s[i] * residual, axis=0, keepdims=True)
        it_ref[i:i + 1, :] = v_one[i:i + 1, 0:agg_count] + update
    for copy in w_sent + p_sent + v_sent:
        copy.wait_send()


def body(n_fine, n_coarse, fine_blocks, fine_columns, coarse_slots, ghost_lists, tentative, members, coarse_columns,
         coarse_rhs, coarse_guess):
    fine_rows, order, _, cells = fine_blocks.shape
    slots, agg_count = coarse_columns.shape
    rest = fine_rows - 1
    ghosts = ghost_lists.reshape(-1, LANES)
    rows = -(-order * order // 16) * 16
    vm = pltpu.VMEM
    scratch = [
        vm((order, order, fine_rows, cells), F32), vm(fine_columns.shape, jnp.int32), vm(coarse_slots.shape, jnp.int32),
        vm(ghosts.shape, jnp.int32), vm(tentative.shape, F32), vm(members.shape, jnp.int32),
        vm(coarse_columns.shape, jnp.int32), vm(coarse_rhs.shape, F32), vm(coarse_guess.shape, F32),
        vm((16, agg_count), F32), vm((16, agg_count), F32),
        vm((16, LANES), F32), vm((16, LANES), F32), vm((16, LANES), F32),
        vm((cells, agg_count), BF16), vm((agg_count, cells), BF16),
        vm((16, cells), F32), vm((16, cells), F32), vm((16, cells), F32),
        vm((rows, cells), F32), vm((rows, cells), F32), vm((rows, cells), F32),
        vm((order, order, fine_rows, cells), F32), vm((order, 16, cells), F32), vm((order, 16, agg_count), F32),
        vm((4, 8, cells), jnp.int32), vm((8, LANES), jnp.int32),
        vm((cells, rest * cells), BF16), vm((cells, rest * cells), BF16), vm((cells, rest * cells), BF16),
        vm((2 * rows, cells), BF16), vm((32, cells), BF16), vm((16, rest * cells), F32),
        vm((cells // LANES * LANES, LANES), F32),
        vm((rows, rest * cells), F32),
        vm((cells // LANES * rows * 8, LANES), F32), vm((cells // LANES * rows * 8, LANES), F32),
        vm((16, cells), F32), vm((2 * rows, rest * cells), BF16), vm((rest * agg_count, rest * cells), BF16),
        vm((order * order * 8, LANES), F32),
        pltpu.SemaphoreType.DMA((9,)), pltpu.SemaphoreType.DMA((6,)), pltpu.SemaphoreType.DMA((6,)),
    ]
    op, iterate = pl.pallas_call(
        functools.partial(kernel, n_fine, n_coarse),
        out_shape=(jax.ShapeDtypeStruct((order, order, slots, agg_count), F32),
                   jax.ShapeDtypeStruct((order, agg_count), F32)),
        in_specs=[pl.BlockSpec(memory_space=pl.ANY)] * 9,
        out_specs=[pl.BlockSpec(memory_space=pltpu.VMEM)] * 2,
        scratch_shapes=scratch,
        compiler_params=pltpu.CompilerParams(collective_id=0, has_side_effects=True, vmem_limit_bytes=56 * 2**20),
    )(jnp.transpose(fine_blocks, (1, 2, 0, 3)), fine_columns, coarse_slots, ghosts, tentative, members, coarse_columns,
      coarse_rhs, coarse_guess)
    return jnp.transpose(op, (2, 0, 1, 3)), iterate


def solution(mesh):
    both = ("fine", "coarse")
    placed = (
        P(None, None, None, both), P(None, both), P(None, both), P(both), P(None, None, both), P(None, both),
        P(None, both), P(None, both), P(None, both),
    )
    return jax.shard_map(
        functools.partial(body, mesh.shape["fine"], mesh.shape["coarse"]),
        mesh=mesh,
        in_specs=placed,
        out_specs=(P(None, None, None, both), P(None, both)),
        check_vma=False,
    )
```

```python
import functools

import jax
import jax.numpy as jnp
from jax import lax
from jax.experimental import pallas as pl
from jax.experimental.pallas import tpu as pltpu
from jax.sharding import PartitionSpec as P

F32 = jnp.float32
BF16 = jnp.bfloat16
MESH = pl.DeviceIdType.MESH
LANES = 128


def lane_gather(table, index):
    return jnp.take_along_axis(table, index, axis=1, mode="promise_in_bounds")


def halves(value):
    high = value.astype(BF16)
    low = (value - high.astype(F32)).astype(BF16)
    return high, low


def dot_nn(left, right):
    return lax.dot_general(left, right, (((1,), (0,)), ((), ())), preferred_element_type=F32)


def dot_nt(left, right):
    return lax.dot_general(left, right, (((1,), (1,)), ((), ())), preferred_element_type=F32)


def kernel(
    n_fine, n_coarse,
    a_hbm, col_hbm, slot_hbm, ghost_hbm, p_hbm, mem_hbm, rhs_hbm, guess_hbm,
    op_s, small_s,
    a_v, col_v, slot_v, ghost_v, p_v, mem_v, rhs_v, guess_v,
    v_pad, v_one, v_near, v_far,
    mt_s, m_s, w_own, w_near, w_far, pc_own, pc_near, pc_far,
    q_s, d_s, idx_s, oh_own, oh_near, oh_far,
    phl_s, whl_s, wacc_s, wg_s, acc_s, g_s, prod_s, z_s, lhs_s, rt_s,
    in_sem, send_sem, recv_sem,
):
    n_all = n_fine * n_coarse
    me = lax.axis_index("fine") * n_coarse + lax.axis_index("coarse")
    odd = lax.rem(me, 2)
    near = me + 1 - 2 * odd
    far = lax.rem(me + n_all - 1 + 2 * odd, n_all)
    near_id = (near // n_coarse, lax.rem(near, n_coarse))
    far_id = (far // n_coarse, lax.rem(far, n_coarse))

    has_far = jnp.logical_and(jnp.logical_or(odd == 1, me > 0), jnp.logical_or(odd == 0, me < n_all - 1))
    early = lax.rem(me, 8 * n_coarse) == 0

    barrier = pltpu.get_barrier_semaphore()

    @pl.when(has_far)
    def greet():
        pl.semaphore_signal(barrier, inc=1, device_id=far_id, device_id_type=MESH)

    pl.semaphore_signal(barrier, inc=1, device_id=near_id, device_id_type=MESH)

    order, agg_count = rhs_v.shape
    slots = 1 + rt_s.shape[0] // agg_count
    fine_rows = a_v.shape[2]
    cells = p_v.shape[2]
    tiles = cells // LANES
    rows = pc_own.shape[0]
    span = rows * 8
    rest = fine_rows - 1

    pairs = [(p_hbm, p_v), (mem_hbm, mem_v), (guess_hbm, guess_v), (col_hbm, col_v), (ghost_hbm, ghost_v),
             (slot_hbm, slot_v), (rhs_hbm, rhs_v)]
    pairs += [(a_hbm.at[:, 2 * b:2 * b + 2], a_v.at[:, 2 * b:2 * b + 2]) for b in range(order // 2)]
    loads = [pltpu.make_async_copy(src, dst, in_sem.at[i]) for i, (src, dst) in enumerate(pairs)]
    for load in loads:
        load.start()

    loads[1].wait()
    cell_row = lax.broadcasted_iota(jnp.int32, (cells, agg_count), 0)
    found = None
    for place in range(mem_v.shape[0]):
        hit = cell_row == mem_v[place:place + 1, :]
        found = hit if found is None else jnp.logical_or(found, hit)
    mt_s[...] = jnp.where(found, 1.0, 0.0).astype(BF16)
    eye = jnp.where(
        lax.broadcasted_iota(jnp.int32, (agg_count, agg_count), 0)
        == lax.broadcasted_iota(jnp.int32, (agg_count, agg_count), 1), 1.0, 0.0).astype(BF16)
    m_s[...] = dot_nt(eye, mt_s[...]).astype(BF16)

    loads[2].wait()
    v_pad[...] = jnp.zeros_like(v_pad)
    v_pad[0:order, :] = guess_v[...]
    high, low = halves(v_pad[...])
    v_cells = (dot_nn(high, m_s[...]) + dot_nn(low, m_s[...]))[0:order, :]
    loads[0].wait()
    w_own[...] = jnp.zeros_like(w_own)
    for j in range(order):
        w_own[j:j + 1, :] = jnp.sum(p_v[j] * v_cells, axis=0, keepdims=True)
    pc_own[...] = jnp.zeros_like(pc_own)
    for j in range(order):
        pc_own[order * j:order * (j + 1), :] = p_v[j]

    def exchange(source, to_near, to_far, base):
        return [pltpu.make_async_remote_copy(
            src_ref=source, dst_ref=dst, send_sem=send_sem.at[base + at], recv_sem=recv_sem.at[base + at],
            device_id=ident, device_id_type=MESH)
            for at, (dst, ident) in enumerate(((to_far, far_id), (to_near, near_id)))]

    def launch(copies):
        @pl.when(has_far)
        def start_far():
            copies[0].start()

        copies[1].start()

    def await_far(copy, landing):
        @pl.when(has_far)
        def take():
            copy.wait_recv()

        @pl.when(jnp.logical_not(has_far))
        def clear():
            landing[...] = jnp.zeros_like(landing)

    w_sent = exchange(w_own, w_near, w_far, 0)
    p_sent = exchange(pc_own, pc_near, pc_far, 2)
    v_sent = exchange(v_one, v_near, v_far, 4)

    def handshake():
        pl.semaphore_wait(barrier, 1 + has_far.astype(jnp.int32))
        launch(w_sent)
        launch(p_sent)

    @pl.when(jnp.logical_not(early))
    def greet_now():
        handshake()

    def q_step(step, carry):
        pair = step // tiles

        @pl.when(lax.rem(step, tiles) == 0)
        def arrive():
            pltpu.make_async_copy(a_hbm.at[:, pl.ds(pair * 2, 2)], a_v.at[:, pl.ds(pair * 2, 2)], in_sem.at[7 + pair]).wait()

        lanes = pl.ds(pl.multiple_of(lax.rem(step, tiles) * LANES, LANES), LANES)
        blocks = [[a_v[r, pair * 2 + jj, :, lanes] for r in range(order)] for jj in range(2)]
        for i in range(order):
            total = [None, None]
            for r in range(order):
                basis = p_v[r, i:i + 1, lanes]
                for jj in range(2):
                    term = basis * blocks[jj][r]
                    total[jj] = term if total[jj] is None else total[jj] + term
            for jj in range(2):
                q_s[i, pair * 2 + jj, :, lanes] = total[jj]
        return carry

    lax.fori_loop(0, order // 2 * tiles, q_step, 0)

    d_s[...] = jnp.zeros_like(d_s)

    def d_step(i, carry):
        total = None
        for j in range(order):
            term = q_s[i, j, 0:1, :] * p_v[j]
            total = term if total is None else total + term
        d_s[i, 0:order, :] = total
        return carry

    lax.fori_loop(0, order, d_step, 0)
    deep = d_s.shape[1]
    high, low = halves(d_s[...].reshape(order * deep, cells))
    diagonal = (dot_nt(high, m_s[...]) + dot_nt(low, m_s[...])).reshape(order, deep, agg_count)
    wide = jnp.zeros((order, LANES - agg_count), F32)
    for i in range(order):
        op_s[pl.ds(i * order * 8, order, stride=8), :] = jnp.concatenate([diagonal[i, 0:order, :], wide], axis=1)
    inverse = jnp.stack([op_s[pl.ds(l * 8, order, stride=order * 8), :][:, 0:agg_count] for l in range(order)])
    entry = lax.broadcasted_iota(jnp.int32, (order, agg_count), 0)
    row_at = lax.broadcasted_iota(jnp.int32, (order, 1, agg_count), 0)
    for pivot in range(order):
        line = inverse[pivot]
        scale = 1.0 / line[pivot:pivot + 1, :]
        line = jnp.where(entry == pivot, 1.0, line) * scale
        factor = inverse[:, pivot:pivot + 1, :]
        kept = jnp.where((entry == pivot)[None], 0.0, inverse)
        inverse = kept - factor * line[None]
        inverse = jnp.where(row_at == pivot, line[None], inverse)
    for i in range(order):
        small_s[16 * i + 32:16 * i + 32 + order, 0:agg_count] = inverse[i]

    loads[3].wait()
    loads[4].wait()
    idx_s[...] = jnp.zeros_like(idx_s)
    idx_s[0, 0:fine_rows, :] = col_v[...]
    is_odd = jnp.full((8, LANES), odd, jnp.int32)
    half = ghost_v.shape[0] * LANES // 2
    for t in range(tiles):
        at = slice(t * LANES, (t + 1) * LANES)
        col = idx_s[0, :, at]
        place = jnp.maximum(col - cells, 0)
        lane = jnp.bitwise_and(place, LANES - 1)
        part = jnp.right_shift(place, 7)
        cell = jnp.zeros((8, LANES), jnp.int32)
        for b in range(ghost_v.shape[0]):
            got = lane_gather(jnp.broadcast_to(ghost_v[b:b + 1, :], (8, LANES)), lane)
            cell = jnp.where(part == b, got, cell)
        own = col < cells
        after = jnp.where(col >= cells + half, 1, 0)
        same = after != is_odd
        idx_s[1, :, at] = jnp.where(own, col, -1)
        idx_s[2, :, at] = jnp.where(jnp.logical_and(jnp.logical_not(own), same), cell, -1)
        idx_s[3, :, at] = jnp.where(jnp.logical_or(own, same), -1, cell)
    ramp = lax.broadcasted_iota(jnp.int32, (256, cells), 0).astype(F32).astype(BF16)
    one = jnp.ones((256, cells), BF16)
    zero = jnp.zeros((256, cells), BF16)
    for group, hot in ((1, oh_own), (2, oh_near), (3, oh_far)):
        for k in range(rest):
            for block in range(cells // 256):
                line = (idx_s[group, k + 1:k + 2, :] - 256 * block).astype(F32).astype(BF16)
                hot[256 * block:256 * (block + 1), k * cells:(k + 1) * cells] = jnp.where(ramp == line, one, zero)

    loads[5].wait()
    member = m_s[...]
    none = jnp.zeros_like(member)
    for k in range(rest):
        line = slot_v[k + 1:k + 2, :].astype(F32).astype(BF16)
        wide_line = jnp.broadcast_to(line, (agg_count, cells))
        for s in range(1, slots):
            picked = wide_line == jnp.full((agg_count, cells), s, BF16)
            rt_s[(s - 1) * agg_count:s * agg_count, k * cells:(k + 1) * cells] = jnp.where(picked, member, none)

    def split_basis(source):
        high, low = halves(source[...])
        phl_s[0:rows, :] = high
        phl_s[rows:2 * rows, :] = low

    def basis_part(hot, k):
        both = dot_nn(phl_s[...], hot[:, k * cells:(k + 1) * cells])
        return both[0:rows, :] + both[rows:2 * rows, :]

    def vector_part(source, hot, k):
        both = dot_nn(whl_s[...], hot[:, k * cells:(k + 1) * cells])
        return both[0:16, :] + both[16:32, :]

    def split_vector(source):
        high, low = halves(source[...])
        whl_s[0:16, :] = high
        whl_s[16:32, :] = low

    split_vector(w_own)
    for k in range(rest):
        wacc_s[:, k * cells:(k + 1) * cells] = vector_part(w_own, oh_own, k)

    def own_basis():
        split_basis(pc_own)
        for k in range(rest):
            acc_s[:, k * cells:(k + 1) * cells] = basis_part(oh_own, k)

    @pl.when(early)
    def greet_late():
        own_basis()
        handshake()

    w_sent[1].wait_recv()
    split_vector(w_near)
    for k in range(rest):
        wacc_s[:, k * cells:(k + 1) * cells] += vector_part(w_near, oh_near, k)
    for t in range(tiles):
        wg_s[pl.ds(t * LANES, 16, stride=8), :] = w_own[:, t * LANES:(t + 1) * LANES]
    loads[6].wait()
    await_far(w_sent[0], w_far)

    split_vector(w_far)
    for k in range(rest):
        total = wacc_s[:, k * cells:(k + 1) * cells] + vector_part(w_far, oh_far, k)
        for t in range(tiles):
            wg_s[pl.ds(t * LANES + k + 1, 16, stride=8), :] = total[:, t * LANES:(t + 1) * LANES]

    for t in range(tiles):
        at = slice(t * LANES, (t + 1) * LANES)
        taken = [wg_s[t * LANES + j * 8:t * LANES + j * 8 + fine_rows, :] for j in range(order)]
        for i in range(order):
            total = None
            for j in range(order):
                term = q_s[i, j, :, at] * taken[j]
                total = term if total is None else total + term
            z_s[8 * i:8 * i + fine_rows, at] = total

    high, low = halves(z_s[...])
    applied = dot_nt(high, m_s[...]) + dot_nt(low, m_s[...])
    update = v_pad[0:order, :]
    for j in range(order):
        line = rhs_v[j:j + 1, :] - jnp.sum(applied[8 * j:8 * j + fine_rows], axis=0, keepdims=True)
        update = update + small_s[16 * j + 32:16 * j + 32 + order, 0:agg_count] * line
    v_one[...] = jnp.zeros_like(v_one)
    v_one[0:order, 0:agg_count] = update
    launch(v_sent)

    @pl.when(jnp.logical_not(early))
    def own_late():
        own_basis()

    p_sent[1].wait_recv()
    split_basis(pc_near)
    for k in range(rest):
        acc_s[:, k * cells:(k + 1) * cells] += basis_part(oh_near, k)
    await_far(p_sent[0], pc_far)

    split_basis(pc_far)
    for k in range(rest):
        total = acc_s[:, k * cells:(k + 1) * cells] + basis_part(oh_far, k)
        for t in range(tiles):
            g_s[pl.ds(t * span + k + 1, rows, stride=8), :] = total[:, t * LANES:(t + 1) * LANES]

    def product_step(step, carry):
        pair = step // tiles
        t = lax.rem(step, tiles)
        lanes = pl.ds(pl.multiple_of(t * LANES, LANES), LANES)
        base = t * span + pair * 16
        taken = [[g_s[pl.ds(pl.multiple_of(base + (j * order + ll) * 8, 8), fine_rows), :] for j in range(order)]
                 for ll in range(2)]
        for i in range(order):
            total = [None, None]
            for j in range(order):
                left = q_s[i, j, :, lanes]
                for ll in range(2):
                    term = left * taken[ll][j]
                    total[ll] = term if total[ll] is None else total[ll] + term
            for ll in range(2):
                prod_s[pl.ds(pl.multiple_of(base + (i * order + ll) * 8, 8), fine_rows), :] = total[ll]
        return carry

    lax.fori_loop(0, order // 2 * tiles, product_step, 0)
    for k in range(rest):
        for t in range(tiles):
            high, low = halves(prod_s[pl.ds(t * span + k + 1, rows, stride=8), :])
            at = slice(k * cells + t * LANES, k * cells + (t + 1) * LANES)
            lhs_s[0:rows, at] = high
            lhs_s[rows:2 * rows, at] = low
    both = dot_nt(lhs_s[...], rt_s[...])
    summed = both[0:rows, :] + both[rows:2 * rows, :]
    filler = jnp.zeros((order * order, LANES - agg_count), F32)
    for s in range(1, slots):
        part = summed[0:order * order, (s - 1) * agg_count:s * agg_count]
        op_s[pl.ds(s, order * order, stride=8), :] = jnp.concatenate([part, filler], axis=1)

    v_sent[1].wait_recv()
    small_s[0:16, :] = jnp.concatenate([v_one[:, 0:agg_count], v_near[:, 0:agg_count]], axis=1)
    await_far(v_sent[0], v_far)
    small_s[16:32, :] = v_far[...]
    for copies in (w_sent, p_sent, v_sent):
        copies[1].wait_send()

        @pl.when(has_far)
        def drain():
            copies[0].wait_send()


def finish(n_fine, n_coarse, op_s, small_s, cc_v, rhs_v, op_ref, it_ref, cc_s):
    odd = lax.rem(lax.axis_index("coarse"), 2)
    is_odd = jnp.full((8, LANES), odd, jnp.int32)
    order, agg_count = rhs_v.shape
    slots = cc_v.shape[0]
    cc_s[...] = jnp.zeros_like(cc_s)
    cc_s[0:slots, 0:agg_count] = cc_v[...]
    column = cc_s[...]
    lane = jnp.bitwise_and(column, agg_count - 1)
    holder = column // agg_count
    is_near = holder == 2 - 2 * is_odd
    is_far = holder == 2 * is_odd
    first = lane + jnp.where(is_near, agg_count, 0)
    names = []
    for l in range(order):
        one_side = lane_gather(jnp.broadcast_to(small_s[l:l + 1, :], (8, LANES)), first)
        other = lane_gather(jnp.broadcast_to(small_s[16 + l:17 + l, :], (8, LANES)), lane)
        names.append(jnp.where(is_far, other, one_side)[0:slots, 0:agg_count])
    update = small_s[0:order, 0:agg_count]
    for i in range(order):
        total = None
        for l in range(order):
            block = op_s[(i * order + l) * 8:(i * order + l) * 8 + slots, 0:agg_count]
            op_ref[i, l] = block
            term = block * names[l]
            total = term if total is None else total + term
        line = rhs_v[i:i + 1, :] - jnp.sum(total, axis=0, keepdims=True)
        update = update + small_s[16 * i + 32:16 * i + 32 + order, 0:agg_count] * line
    it_ref[...] = update


def body(n_fine, n_coarse, fine_blocks, fine_columns, coarse_slots, ghost_lists, tentative, members, coarse_columns,
         coarse_rhs, coarse_guess):
    fine_rows, order, _, cells = fine_blocks.shape
    slots, agg_count = coarse_columns.shape
    rest = fine_rows - 1
    ghosts = ghost_lists.reshape(-1, LANES)
    rows = -(-order * order // 16) * 16
    vm = pltpu.VMEM
    scratch = [
        vm((order, order, fine_rows, cells), F32), vm(fine_columns.shape, jnp.int32), vm(coarse_slots.shape, jnp.int32),
        vm(ghosts.shape, jnp.int32), vm(tentative.shape, F32), vm(members.shape, jnp.int32),
        vm(coarse_rhs.shape, F32), vm(coarse_guess.shape, F32),
        vm((16, agg_count), F32),
        vm((16, LANES), F32), vm((16, LANES), F32), vm((16, LANES), F32),
        vm((cells, agg_count), BF16), vm((agg_count, cells), BF16),
        vm((16, cells), F32), vm((16, cells), F32), vm((16, cells), F32),
        vm((rows, cells), F32), vm((rows, cells), F32), vm((rows, cells), F32),
        vm((order, order, fine_rows, cells), F32), vm((order, 16, cells), F32),
        vm((4, 8, cells), jnp.int32),
        vm((cells, rest * cells), BF16), vm((cells, rest * cells), BF16), vm((cells, rest * cells), BF16),
        vm((2 * rows, cells), BF16), vm((32, cells), BF16), vm((16, rest * cells), F32),
        vm((cells // LANES * LANES, LANES), F32),
        vm((rows, rest * cells), F32),
        vm((cells // LANES * rows * 8, LANES), F32), vm((cells // LANES * rows * 8, LANES), F32),
        vm((8 * order, cells), F32), vm((2 * rows, rest * cells), BF16), vm(((slots - 1) * agg_count, rest * cells), BF16),
        pltpu.SemaphoreType.DMA((7 + order // 2,)), pltpu.SemaphoreType.DMA((6,)), pltpu.SemaphoreType.DMA((6,)),
    ]
    in_vmem = pl.BlockSpec(memory_space=pltpu.VMEM)
    padded, small = pl.pallas_call(
        functools.partial(kernel, n_fine, n_coarse),
        out_shape=(vm((order * order * 8, LANES), F32), vm((16 * order + 32, LANES), F32)),
        in_specs=[pl.BlockSpec(memory_space=pltpu.HBM)] * 8,
        out_specs=[in_vmem] * 2,
        scratch_shapes=scratch,
        compiler_params=pltpu.CompilerParams(collective_id=0, has_side_effects=True, vmem_limit_bytes=40 * 2**20),
    )(*[pltpu.with_memory_space_constraint(given, pltpu.HBM) for given in (
        jnp.transpose(fine_blocks, (1, 2, 0, 3)), fine_columns, coarse_slots, ghosts, tentative, members, coarse_rhs,
        coarse_guess)])
    op, iterate = pl.pallas_call(
        functools.partial(finish, n_fine, n_coarse),
        out_shape=(jax.ShapeDtypeStruct((order, order, slots, agg_count), F32),
                   jax.ShapeDtypeStruct((order, agg_count), F32)),
        in_specs=[in_vmem] * 4,
        out_specs=[in_vmem] * 2,
        scratch_shapes=[vm((8, LANES), jnp.int32)],
        compiler_params=pltpu.CompilerParams(vmem_limit_bytes=8 * 2**20),
    )(padded, small, coarse_columns, coarse_rhs)
    return jnp.transpose(op, (2, 0, 1, 3)), iterate


def solution(mesh):
    both = ("fine", "coarse")
    placed = (
        P(None, None, None, both), P(None, both), P(None, both), P(both), P(None, None, both), P(None, both),
        P(None, both), P(None, both), P(None, both),
    )
    return jax.shard_map(
        functools.partial(body, mesh.shape["fine"], mesh.shape["coarse"]),
        mesh=mesh,
        in_specs=placed,
        out_specs=(P(None, None, None, both), P(None, both)),
        check_vma=False,
    )
```

```python
import functools

import jax
import jax.numpy as jnp
from jax import lax
from jax.experimental import pallas as pl
from jax.experimental.pallas import tpu as pltpu
from jax.sharding import PartitionSpec as P

F32 = jnp.float32
BF16 = jnp.bfloat16
MESH = pl.DeviceIdType.MESH
LANES = 128


def lane_gather(table, index):
    return jnp.take_along_axis(table, index, axis=1, mode="promise_in_bounds")


def column_parts(order):
    return (0,), (order,)


def halves(value):
    high = value.astype(BF16)
    low = (value - high.astype(F32)).astype(BF16)
    return high, low


def dot_nn(left, right):
    return lax.dot_general(left, right, (((1,), (0,)), ((), ())), preferred_element_type=F32)


def dot_nt(left, right):
    return lax.dot_general(left, right, (((1,), (1,)), ((), ())), preferred_element_type=F32)


def kernel(
    n_fine, n_coarse,
    a_hbm, col_hbm, slot_hbm, ghost_hbm, p_hbm, mem_hbm, rhs_hbm, guess_hbm,
    op_s, small_s,
    a_v, col_v, slot_v, ghost_v, p_v, mem_v, rhs_v, guess_v,
    v_pad, v_one, v_near, v_far,
    mt_s, m_s, w_own, w_near, w_far, w_held, pc_own, pc_near, pc_far,
    q_s, ap_s, d_s, idx_s, oh_own, oh_near, oh_far,
    phl_s, whl_s, wacc_s, wg_s, acc_s, g_s, prod_s, z_s, lhs_s, rt_s,
    in_sem, send_sem, recv_sem, met_sem,
):
    n_all = n_fine * n_coarse
    me = lax.axis_index("fine") * n_coarse + lax.axis_index("coarse")
    odd = lax.rem(me, 2)
    near = me + 1 - 2 * odd
    far = lax.rem(me + n_all - 1 + 2 * odd, n_all)
    near_id = (near // n_coarse, lax.rem(near, n_coarse))
    far_id = (far // n_coarse, lax.rem(far, n_coarse))

    has_far = jnp.logical_and(jnp.logical_or(odd == 1, me > 0), jnp.logical_or(odd == 0, me < n_all - 1))
    lap = 8 * n_coarse
    heads = jnp.logical_and(lax.rem(me, lap) == 0, me > 0)
    tails = jnp.logical_and(lax.rem(me, lap) == lap - 1, me < n_all - 1)
    bridges = jnp.logical_and(lax.rem(me, lap) == n_coarse - 1, me < n_all - lap)
    lap_head = lax.rem((me // lap + 1) * lap, n_all)
    head_id = (lap_head // n_coarse, lax.rem(lap_head, n_coarse))
    lap_tail = (me // lap + 1) * lap - 1
    tail_id = (lap_tail // n_coarse, lax.rem(lap_tail, n_coarse))
    bridge = jnp.where(heads, me - lap, me // lap * lap) + n_coarse - 1
    bridge_id = (bridge // n_coarse, lax.rem(bridge, n_coarse))
    lazy = me == 1

    barrier = pltpu.get_barrier_semaphore()

    @pl.when(jnp.logical_and(has_far, jnp.logical_not(tails)))
    def greet():
        pl.semaphore_signal(barrier, inc=1, device_id=far_id, device_id_type=MESH)

    pl.semaphore_signal(barrier, inc=1, device_id=near_id, device_id_type=MESH)

    @pl.when(bridges)
    def greet_lap():
        pl.semaphore_signal(barrier, inc=1, device_id=tail_id, device_id_type=MESH)
        pl.semaphore_signal(barrier, inc=1, device_id=head_id, device_id_type=MESH)

    order, agg_count = rhs_v.shape
    slots = 1 + rt_s.shape[0] // agg_count
    fine_rows = a_v.shape[2]
    cells = p_v.shape[2]
    tiles = cells // LANES
    firsts, counts = column_parts(order)
    sent = [-(-count * order // 8) * 8 for count in counts]
    tall = [-(-count * order // 16) * 16 for count in counts]
    at_row = (0,)
    op_row = (0,)
    parts = len(counts)
    span = prod_s.shape[0] // tiles
    rest = fine_rows - 1

    pairs = [(p_hbm, p_v), (mem_hbm, mem_v), (guess_hbm, guess_v), (col_hbm, col_v), (ghost_hbm, ghost_v),
             (slot_hbm, slot_v), (rhs_hbm, rhs_v)]
    pairs += [(a_hbm.at[:, 2 * b:2 * b + 2], a_v.at[:, 2 * b:2 * b + 2]) for b in range(order // 2)]
    loads = [pltpu.make_async_copy(src, dst, in_sem.at[i]) for i, (src, dst) in enumerate(pairs)]
    for load in loads:
        load.start()

    def exchange(source, to_near, to_far, base):
        return [pltpu.make_async_remote_copy(
            src_ref=source, dst_ref=dst, send_sem=send_sem.at[base + at], recv_sem=recv_sem.at[base + at],
            device_id=ident, device_id_type=MESH)
            for at, (dst, ident) in enumerate(((to_far, far_id), (to_near, near_id)))]

    def launch_far(copies):
        @pl.when(has_far)
        def start_far():
            copies[0].start()

    def await_far(copy, landing):
        @pl.when(has_far)
        def take():
            copy.wait_recv()

        @pl.when(jnp.logical_not(has_far))
        def clear():
            landing[...] = jnp.zeros_like(landing)

    w_sent = exchange(w_own, w_near, w_far, 0)
    v_sent = exchange(v_one, v_near, v_far, 2)
    p_sent = [exchange(*(ref.at[at_row[c]:at_row[c] + sent[c]] for ref in (pc_own, pc_near, pc_far)), 4 + 2 * c)
              for c in range(parts)]
    w_up = pltpu.make_async_remote_copy(
        src_ref=w_own, dst_ref=w_held, send_sem=send_sem.at[8], recv_sem=recv_sem.at[8],
        device_id=bridge_id, device_id_type=MESH)
    w_over = pltpu.make_async_remote_copy(
        src_ref=w_held, dst_ref=w_far, send_sem=send_sem.at[9], recv_sem=recv_sem.at[0],
        device_id=tail_id, device_id_type=MESH)

    def await_barrier():
        pl.semaphore_wait(barrier, 1 + has_far.astype(jnp.int32) + tails.astype(jnp.int32))

    def send_basis():
        for copies in p_sent:
            @pl.when(jnp.logical_not(heads))
            def start_now():
                launch_far(copies)

            copies[1].start()

    def send_vector():
        @pl.when(jnp.logical_not(heads))
        def start_direct():
            launch_far(w_sent)

        @pl.when(heads)
        def start_up():
            w_up.start()

        w_sent[1].start()

    loads[0].wait()
    pc_own[...] = jnp.zeros_like(pc_own)
    for c in range(parts):
        for j in range(order):
            spot = at_row[c] + counts[c] * j
            pc_own[spot:spot + counts[c], :] = p_v[j, firsts[c]:firsts[c] + counts[c], :]

    @pl.when(jnp.logical_not(lazy))
    def meet():
        await_barrier()

        @pl.when(tails)
        def announce():
            pl.semaphore_signal(met_sem, inc=1, device_id=bridge_id, device_id_type=MESH)
            pl.semaphore_signal(met_sem, inc=1, device_id=far_id, device_id_type=MESH)

    loads[1].wait()
    cell_row = lax.broadcasted_iota(jnp.int32, (cells, agg_count), 0)
    found = None
    for place in range(mem_v.shape[0]):
        hit = cell_row == mem_v[place:place + 1, :]
        found = hit if found is None else jnp.logical_or(found, hit)
    mt_s[...] = jnp.where(found, 1.0, 0.0).astype(BF16)
    eye = jnp.where(
        lax.broadcasted_iota(jnp.int32, (agg_count, agg_count), 0)
        == lax.broadcasted_iota(jnp.int32, (agg_count, agg_count), 1), 1.0, 0.0).astype(BF16)
    m_s[...] = dot_nt(eye, mt_s[...]).astype(BF16)

    loads[2].wait()
    v_pad[...] = jnp.zeros_like(v_pad)
    v_pad[0:order, :] = guess_v[...]
    high, low = halves(v_pad[...])
    v_cells = (dot_nn(high, m_s[...]) + dot_nn(low, m_s[...]))[0:order, :]
    w_own[...] = jnp.zeros_like(w_own)
    for j in range(order):
        w_own[j:j + 1, :] = jnp.sum(p_v[j] * v_cells, axis=0, keepdims=True)

    @pl.when(jnp.logical_not(lazy))
    def tell():
        send_vector()
        send_basis()

    loads[3].wait()
    loads[4].wait()
    idx_s[...] = jnp.zeros_like(idx_s)
    idx_s[0, 0:fine_rows, :] = col_v[...]
    is_odd = jnp.full((8, LANES), odd, jnp.int32)
    half = ghost_v.shape[0] * LANES // 2
    for t in range(tiles):
        at = slice(t * LANES, (t + 1) * LANES)
        col = idx_s[0, :, at]
        place = jnp.maximum(col - cells, 0)
        lane = jnp.bitwise_and(place, LANES - 1)
        part = jnp.right_shift(place, 7)
        cell = jnp.zeros((8, LANES), jnp.int32)
        for b in range(ghost_v.shape[0]):
            got = lane_gather(jnp.broadcast_to(ghost_v[b:b + 1, :], (8, LANES)), lane)
            cell = jnp.where(part == b, got, cell)
        own = col < cells
        after = jnp.where(col >= cells + half, 1, 0)
        same = after != is_odd
        idx_s[1, :, at] = jnp.where(own, col, -1)
        idx_s[2, :, at] = jnp.where(jnp.logical_and(jnp.logical_not(own), same), cell, -1)
        idx_s[3, :, at] = jnp.where(jnp.logical_or(own, same), -1, cell)
    ramp = lax.broadcasted_iota(jnp.int32, (256, cells), 0).astype(F32).astype(BF16)
    one = jnp.ones((256, cells), BF16)
    zero = jnp.zeros((256, cells), BF16)
    for group, hot in ((1, oh_own), (2, oh_near), (3, oh_far)):
        for k in range(rest):
            for block in range(cells // 256):
                line = (idx_s[group, k + 1:k + 2, :] - 256 * block).astype(F32).astype(BF16)
                hot[256 * block:256 * (block + 1), k * cells:(k + 1) * cells] = jnp.where(ramp == line, one, zero)

    def split_basis(source, c):
        high, low = halves(source[at_row[c]:at_row[c] + tall[c], :])
        phl_s[0:tall[c], 0:cells] = high
        phl_s[0:tall[c], cells:2 * cells] = low

    def basis_part(hot, c, k):
        hot_part = hot[:, k * cells:(k + 1) * cells]
        return dot_nn(phl_s[0:tall[c], :], jnp.concatenate([hot_part, hot_part], axis=0))

    def vector_part(hot, k):
        both = dot_nn(whl_s[...], hot[:, k * cells:(k + 1) * cells])
        return both[0:16, :] + both[16:32, :]

    def split_vector(source):
        high, low = halves(source[...])
        whl_s[0:16, :] = high
        whl_s[16:32, :] = low

    split_vector(w_own)
    for k in range(rest):
        wacc_s[:, k * cells:(k + 1) * cells] = vector_part(oh_own, k)
    for t in range(tiles):
        wg_s[pl.ds(t * LANES, 16, stride=8), :] = w_own[:, t * LANES:(t + 1) * LANES]

    for b in range(order // 2):
        loads[7 + b].wait()
    d_s[...] = jnp.zeros_like(d_s)
    for t in range(tiles):
        at = slice(t * LANES, (t + 1) * LANES)
        for r in range(order):
            total = None
            for j in range(order):
                term = a_v[r, j, 0:1, at] * p_v[j, :, at]
                total = term if total is None else total + term
            ap_s[r, 0:order, :] = total
        for i in range(order):
            total = None
            for r in range(order):
                term = p_v[r, i:i + 1, at] * ap_s[r, 0:order, :]
                total = term if total is None else total + term
            d_s[i, 0:order, at] = total
    deep = d_s.shape[1]
    high, low = halves(d_s[...].reshape(order * deep, cells))
    diagonal = (dot_nt(high, m_s[...]) + dot_nt(low, m_s[...])).reshape(order, deep, agg_count)
    wide = jnp.zeros((order, LANES - agg_count), F32)
    for i in range(order):
        for c in range(parts):
            line = jnp.concatenate([diagonal[i, firsts[c]:firsts[c] + counts[c], :], wide[0:counts[c]]], axis=1)
            op_s[pl.ds((op_row[c] + i * counts[c]) * 8, counts[c], stride=8), :] = line
    inverse = jnp.stack([op_s[pl.ds((op_row[c] + l) * 8, order, stride=counts[c] * 8), :][:, 0:agg_count]
                         for c in range(parts) for l in range(counts[c])])
    entry = lax.broadcasted_iota(jnp.int32, (order, agg_count), 0)
    row_at = lax.broadcasted_iota(jnp.int32, (order, 1, agg_count), 0)
    for pivot in range(order):
        line = inverse[pivot]
        scale = 1.0 / line[pivot:pivot + 1, :]
        line = jnp.where(entry == pivot, 1.0, line) * scale
        factor = inverse[:, pivot:pivot + 1, :]
        kept = jnp.where((entry == pivot)[None], 0.0, inverse)
        inverse = kept - factor * line[None]
        inverse = jnp.where(row_at == pivot, line[None], inverse)
    for i in range(order):
        small_s[16 * i + 32:16 * i + 32 + order, 0:agg_count] = inverse[i]

    loads[6].wait()
    z_s[...] = jnp.zeros_like(z_s)
    v_one[...] = jnp.zeros_like(v_one)

    def sweep():
        w_sent[1].wait_recv()
        split_vector(w_near)
        for k in range(rest):
            wacc_s[:, k * cells:(k + 1) * cells] += vector_part(oh_near, k)

        await_far(w_sent[0], w_far)
        split_vector(w_far)
        for k in range(rest):
            total = wacc_s[:, k * cells:(k + 1) * cells] + vector_part(oh_far, k)
            for t in range(tiles):
                wg_s[pl.ds(t * LANES + k + 1, 16, stride=8), :] = total[:, t * LANES:(t + 1) * LANES]

        for t in range(tiles):
            at = slice(t * LANES, (t + 1) * LANES)
            taken = [wg_s[t * LANES + j * 8:t * LANES + j * 8 + fine_rows, :] for j in range(order)]
            whole = None
            for r in range(order):
                total = None
                for j in range(order):
                    term = a_v[r, j, :, at] * taken[j]
                    total = term if total is None else total + term
                term = p_v[r, :, at] * jnp.sum(total, axis=0, keepdims=True)
                whole = term if whole is None else whole + term
            z_s[0:order, at] = whole

        high, low = halves(z_s[...])
        whl_s[0:16, :] = high
        whl_s[16:32, :] = low
        both = dot_nt(whl_s[...], m_s[...])
        residual = rhs_v[...] - (both[0:order, :] + both[16:16 + order, :])
        update = v_pad[0:order, :]
        for j in range(order):
            update = update + small_s[16 * j + 32:16 * j + 32 + order, 0:agg_count] * residual[j:j + 1, :]
        v_one[0:order, 0:agg_count] = update
        launch_far(v_sent)
        v_sent[1].start()

    def prepare():
        loads[5].wait()
        member = m_s[...]
        none = jnp.zeros_like(member)
        for k in range(rest):
            line = slot_v[k + 1:k + 2, :].astype(F32).astype(BF16)
            wide_line = jnp.broadcast_to(line, (agg_count, cells))
            for s in range(1, slots):
                picked = wide_line == jnp.full((agg_count, cells), s, BF16)
                rt_s[(s - 1) * agg_count:s * agg_count, k * cells:(k + 1) * cells] = jnp.where(picked, member, none)

        def q_step(step, carry):
            pair = step // tiles

            lanes = pl.ds(pl.multiple_of(lax.rem(step, tiles) * LANES, LANES), LANES)
            blocks = [[a_v[r, pair * 2 + jj, :, lanes] for r in range(order)] for jj in range(2)]
            for i in range(order):
                total = [None, None]
                for r in range(order):
                    basis = p_v[r, i:i + 1, lanes]
                    for jj in range(2):
                        term = basis * blocks[jj][r]
                        total[jj] = term if total[jj] is None else total[jj] + term
                for jj in range(2):
                    q_s[i, pair * 2 + jj, :, lanes] = total[jj]
            return carry

        lax.fori_loop(0, order // 2 * tiles, q_step, 0)

        @pl.when(lazy)
        def meet_late():
            await_barrier()
            send_vector()
            send_basis()

        @pl.when(bridges)
        def hand_on():
            w_up.wait_recv()
            pl.semaphore_wait(met_sem, 1)
            w_over.start()

        for c in range(parts):
            split_basis(pc_own, c)
            for k in range(rest):
                acc_s[at_row[c]:at_row[c] + tall[c], k * cells:(k + 1) * cells] = basis_part(oh_own, c, k)
        for c in range(parts):
            p_sent[c][1].wait_recv()
            split_basis(pc_near, c)
            for k in range(rest):
                acc_s[at_row[c]:at_row[c] + tall[c], k * cells:(k + 1) * cells] += basis_part(oh_near, c, k)

        @pl.when(heads)
        def start_late():
            pl.semaphore_wait(met_sem, 1)
            for copies in p_sent:
                copies[0].start()

    def turn(at, carry):
        @pl.when(jnp.logical_xor(at == 0, tails))
        def run_prepare():
            prepare()

        @pl.when(at == 0)
        def run_sweep():
            sweep()

        return carry

    lax.fori_loop(0, 2, turn, 0)

    def product_part(c):
        pairs_here = counts[c] // 2

        def product_step(step, carry):
            pair = step // tiles
            t = lax.rem(step, tiles)
            lanes = pl.ds(pl.multiple_of(t * LANES, LANES), LANES)
            base = t * span + pair * 16
            taken = [[g_s[pl.ds(pl.multiple_of(base + (j * counts[c] + ll) * 8, 8), fine_rows), :]
                      for j in range(order)] for ll in range(2)]
            for i in range(order):
                total = [None, None]
                for j in range(order):
                    left = q_s[i, j, :, lanes]
                    for ll in range(2):
                        term = left * taken[ll][j]
                        total[ll] = term if total[ll] is None else total[ll] + term
                for ll in range(2):
                    prod_s[pl.ds(pl.multiple_of(base + (i * counts[c] + ll) * 8, 8), fine_rows), :] = total[ll]
            return carry

        lax.fori_loop(0, pairs_here * tiles, product_step, 0)

    for c in range(parts):
        await_far(p_sent[c][0], pc_far.at[at_row[c]:at_row[c] + tall[c]])
        split_basis(pc_far, c)
        height = counts[c] * order
        for k in range(rest):
            total = acc_s[at_row[c]:at_row[c] + tall[c], k * cells:(k + 1) * cells] + basis_part(oh_far, c, k)
            for t in range(tiles):
                g_s[pl.ds(t * span + k + 1, height, stride=8), :] = total[0:height, t * LANES:(t + 1) * LANES]
        product_part(c)
        for k in range(rest):
            for t in range(tiles):
                high, low = halves(prod_s[pl.ds(t * span + k + 1, tall[c], stride=8), :])
                at = slice(k * cells + t * LANES, k * cells + (t + 1) * LANES)
                lhs_s[0:tall[c], at] = high
                lhs_s[tall[c]:2 * tall[c], at] = low
        both = dot_nt(lhs_s[0:2 * tall[c], :], rt_s[...])
        summed = both[0:height, :] + both[tall[c]:tall[c] + height, :]
        filler = jnp.zeros((height, LANES - agg_count), F32)
        for s in range(1, slots):
            part = summed[:, (s - 1) * agg_count:s * agg_count]
            op_s[pl.ds(op_row[c] * 8 + s, height, stride=8), :] = jnp.concatenate([part, filler], axis=1)

    v_sent[1].wait_recv()
    small_s[0:16, :] = jnp.concatenate([v_one[:, 0:agg_count], v_near[:, 0:agg_count]], axis=1)
    await_far(v_sent[0], v_far)
    small_s[16:32, :] = v_far[...]
    for copies in [v_sent] + p_sent:
        copies[1].wait_send()

        @pl.when(has_far)
        def drain():
            copies[0].wait_send()

    w_sent[1].wait_send()

    @pl.when(jnp.logical_and(has_far, jnp.logical_not(heads)))
    def drain_direct():
        w_sent[0].wait_send()

    @pl.when(heads)
    def drain_up():
        w_up.wait_send()

    @pl.when(bridges)
    def drain_over():
        w_over.wait_send()


def finish(n_fine, n_coarse, op_s, small_s, cc_v, rhs_v, op_ref, it_ref, cc_s):
    odd = lax.rem(lax.axis_index("coarse"), 2)
    is_odd = jnp.full((8, LANES), odd, jnp.int32)
    order, agg_count = rhs_v.shape
    slots = cc_v.shape[0]
    cc_s[...] = jnp.zeros_like(cc_s)
    cc_s[0:slots, 0:agg_count] = cc_v[...]
    column = cc_s[...]
    lane = jnp.bitwise_and(column, agg_count - 1)
    holder = column // agg_count
    is_near = holder == 2 - 2 * is_odd
    is_far = holder == 2 * is_odd
    first = lane + jnp.where(is_near, agg_count, 0)
    names = []
    for l in range(order):
        one_side = lane_gather(jnp.broadcast_to(small_s[l:l + 1, :], (8, LANES)), first)
        other = lane_gather(jnp.broadcast_to(small_s[16 + l:17 + l, :], (8, LANES)), lane)
        names.append(jnp.where(is_far, other, one_side)[0:slots, 0:agg_count])
    update = small_s[0:order, 0:agg_count]
    for i in range(order):
        total = None
        for l in range(order):
            row = (i * order + l) * 8
            block = op_s[row:row + slots, 0:agg_count]
            op_ref[i, l] = block
            term = block * names[l]
            total = term if total is None else total + term
        line = rhs_v[i:i + 1, :] - jnp.sum(total, axis=0, keepdims=True)
        update = update + small_s[16 * i + 32:16 * i + 32 + order, 0:agg_count] * line
    it_ref[...] = update


def body(n_fine, n_coarse, fine_blocks, fine_columns, coarse_slots, ghost_lists, tentative, members, coarse_columns,
         coarse_rhs, coarse_guess):
    fine_rows, order, _, cells = fine_blocks.shape
    slots, agg_count = coarse_columns.shape
    rest = fine_rows - 1
    ghosts = ghost_lists.reshape(-1, LANES)
    deep = -(-order * order // 16) * 16
    vm = pltpu.VMEM
    scratch = [
        vm((order, order, fine_rows, cells), F32), vm(fine_columns.shape, jnp.int32), vm(coarse_slots.shape, jnp.int32),
        vm(ghosts.shape, jnp.int32), vm(tentative.shape, F32), vm(members.shape, jnp.int32),
        vm(coarse_rhs.shape, F32), vm(coarse_guess.shape, F32),
        vm((16, agg_count), F32),
        vm((16, LANES), F32), vm((16, LANES), F32), vm((16, LANES), F32),
        vm((cells, agg_count), BF16), vm((agg_count, cells), BF16),
        vm((16, cells), F32), vm((16, cells), F32), vm((16, cells), F32), vm((16, cells), F32),
        vm((deep, cells), F32), vm((deep, cells), F32), vm((deep, cells), F32),
        vm((order, order, fine_rows, cells), F32), vm((order, 16, LANES), F32), vm((order, 16, cells), F32),
        vm((4, 8, cells), jnp.int32),
        vm((cells, rest * cells), BF16), vm((cells, rest * cells), BF16), vm((cells, rest * cells), BF16),
        vm((deep, 2 * cells), BF16), vm((32, cells), BF16), vm((16, rest * cells), F32),
        vm((cells // LANES * LANES, LANES), F32),
        vm((deep, rest * cells), F32),
        vm((cells // LANES * deep * 8, LANES), F32), vm((cells // LANES * deep * 8, LANES), F32),
        vm((16, cells), F32), vm((2 * deep, rest * cells), BF16), vm(((slots - 1) * agg_count, rest * cells), BF16),
        pltpu.SemaphoreType.DMA((7 + order // 2,)), pltpu.SemaphoreType.DMA((10,)), pltpu.SemaphoreType.DMA((9,)),
        pltpu.SemaphoreType.REGULAR,
    ]
    in_vmem = pl.BlockSpec(memory_space=pltpu.VMEM)
    padded, small = pl.pallas_call(
        functools.partial(kernel, n_fine, n_coarse),
        out_shape=(vm((order * order * 8, LANES), F32), vm((16 * order + 32, LANES), F32)),
        in_specs=[pl.BlockSpec(memory_space=pltpu.HBM)] * 8,
        out_specs=[in_vmem] * 2,
        scratch_shapes=scratch,
        compiler_params=pltpu.CompilerParams(collective_id=0, has_side_effects=True, vmem_limit_bytes=40 * 2**20),
    )(*[pltpu.with_memory_space_constraint(given, pltpu.HBM) for given in (
        jnp.transpose(fine_blocks, (1, 2, 0, 3)), fine_columns, coarse_slots, ghosts, tentative, members, coarse_rhs,
        coarse_guess)])
    op, iterate = pl.pallas_call(
        functools.partial(finish, n_fine, n_coarse),
        out_shape=(jax.ShapeDtypeStruct((order, order, slots, agg_count), F32),
                   jax.ShapeDtypeStruct((order, agg_count), F32)),
        in_specs=[in_vmem] * 4,
        out_specs=[in_vmem] * 2,
        scratch_shapes=[vm((8, LANES), jnp.int32)],
        compiler_params=pltpu.CompilerParams(vmem_limit_bytes=8 * 2**20),
    )(padded, small, coarse_columns, coarse_rhs)
    return jnp.transpose(op, (2, 0, 1, 3)), iterate


def solution(mesh):
    both = ("fine", "coarse")
    placed = (
        P(None, None, None, both), P(None, both), P(None, both), P(both), P(None, None, both), P(None, both),
        P(None, both), P(None, both), P(None, both),
    )
    return jax.shard_map(
        functools.partial(body, mesh.shape["fine"], mesh.shape["coarse"]),
        mesh=mesh,
        in_specs=placed,
        out_specs=(P(None, None, None, both), P(None, both)),
        check_vma=False,
    )
```

```python
import functools

import jax
import jax.numpy as jnp
from jax import lax
from jax.experimental import pallas as pl
from jax.experimental.pallas import tpu as pltpu
from jax.sharding import PartitionSpec as P

F32 = jnp.float32
BF16 = jnp.bfloat16
MESH = pl.DeviceIdType.MESH
LANES = 128


def lane_gather(table, index):
    return jnp.take_along_axis(table, index, axis=1, mode="promise_in_bounds")


def column_parts(order):
    return (0,), (order,)


def halves(value):
    high = value.astype(BF16)
    low = (value - high.astype(F32)).astype(BF16)
    return high, low


def dot_nn(left, right):
    return lax.dot_general(left, right, (((1,), (0,)), ((), ())), preferred_element_type=F32)


def dot_nt(left, right):
    return lax.dot_general(left, right, (((1,), (1,)), ((), ())), preferred_element_type=F32)


def kernel(
    n_fine, n_coarse,
    a_hbm, col_hbm, slot_hbm, ghost_hbm, p_hbm, mem_hbm, rhs_hbm, guess_hbm,
    op_s, small_s,
    a_v, col_v, slot_v, ghost_v, p_v, mem_v, rhs_v, guess_v,
    v_pad, v_one, v_near, v_far,
    mt_s, m_s, w_own, w_near, w_far, w_held, pc_own, pc_near, pc_far,
    q_s, ap_s, d_s, idx_s, oh_own, oh_near, oh_far,
    phl_s, whl_s, wacc_s, wg_s, acc_s, g_s, prod_s, z_s, lhs_s, rt_s,
    in_sem, send_sem, recv_sem, met_sem,
):
    n_all = n_fine * n_coarse
    me = lax.axis_index("fine") * n_coarse + lax.axis_index("coarse")
    odd = lax.rem(me, 2)
    near = me + 1 - 2 * odd
    far = lax.rem(me + n_all - 1 + 2 * odd, n_all)
    near_id = (near // n_coarse, lax.rem(near, n_coarse))
    far_id = (far // n_coarse, lax.rem(far, n_coarse))

    has_far = jnp.logical_and(jnp.logical_or(odd == 1, me > 0), jnp.logical_or(odd == 0, me < n_all - 1))
    lap = 8 * n_coarse
    heads = jnp.logical_and(lax.rem(me, lap) == 0, me > 0)
    tails = jnp.logical_and(lax.rem(me, lap) == lap - 1, me < n_all - 1)
    bridges = jnp.logical_and(lax.rem(me, lap) == n_coarse - 1, me < n_all - lap)
    lap_head = lax.rem((me // lap + 1) * lap, n_all)
    head_id = (lap_head // n_coarse, lax.rem(lap_head, n_coarse))
    lap_tail = (me // lap + 1) * lap - 1
    tail_id = (lap_tail // n_coarse, lax.rem(lap_tail, n_coarse))
    bridge = jnp.where(heads, me - lap, me // lap * lap) + n_coarse - 1
    bridge_id = (bridge // n_coarse, lax.rem(bridge, n_coarse))
    lazy = me == 1

    barrier = pltpu.get_barrier_semaphore()

    @pl.when(jnp.logical_and(has_far, jnp.logical_not(tails)))
    def greet():
        pl.semaphore_signal(barrier, inc=1, device_id=far_id, device_id_type=MESH)

    pl.semaphore_signal(barrier, inc=1, device_id=near_id, device_id_type=MESH)

    @pl.when(bridges)
    def greet_lap():
        pl.semaphore_signal(barrier, inc=1, device_id=tail_id, device_id_type=MESH)
        pl.semaphore_signal(barrier, inc=1, device_id=head_id, device_id_type=MESH)

    order, agg_count = rhs_v.shape
    slots = 1 + rt_s.shape[0] // agg_count
    fine_rows = a_v.shape[2]
    cells = p_v.shape[2]
    tiles = cells // LANES
    firsts, counts = column_parts(order)
    sent = [-(-count * order // 8) * 8 for count in counts]
    tall = [-(-count * order // 16) * 16 for count in counts]
    at_row = (0,)
    op_row = (0,)
    parts = len(counts)
    span = prod_s.shape[0] // tiles
    rest = fine_rows - 1

    pairs = [(p_hbm, p_v), (mem_hbm, mem_v), (guess_hbm, guess_v), (col_hbm, col_v), (ghost_hbm, ghost_v),
             (slot_hbm, slot_v), (rhs_hbm, rhs_v)]
    pairs += [(a_hbm.at[:, 2 * b:2 * b + 2], a_v.at[:, 2 * b:2 * b + 2]) for b in range(order // 2)]
    loads = [pltpu.make_async_copy(src, dst, in_sem.at[i]) for i, (src, dst) in enumerate(pairs)]
    for load in loads:
        load.start()

    def exchange(source, to_near, to_far, base):
        return [pltpu.make_async_remote_copy(
            src_ref=source, dst_ref=dst, send_sem=send_sem.at[base + at], recv_sem=recv_sem.at[base + at],
            device_id=ident, device_id_type=MESH)
            for at, (dst, ident) in enumerate(((to_far, far_id), (to_near, near_id)))]

    def launch_far(copies):
        @pl.when(has_far)
        def start_far():
            copies[0].start()

    def await_far(copy, landing):
        @pl.when(has_far)
        def take():
            copy.wait_recv()

        @pl.when(jnp.logical_not(has_far))
        def clear():
            landing[...] = jnp.zeros_like(landing)

    w_sent = exchange(w_own, w_near, w_far, 0)
    v_sent = exchange(v_one, v_near, v_far, 2)
    pieces = ((0, 48), (48, sent[0]))
    p_sent = [exchange(*(ref.at[a:b] for ref in (pc_own, pc_near, pc_far)), 4 + 2 * n)
              for n, (a, b) in enumerate(pieces)]
    w_up = pltpu.make_async_remote_copy(
        src_ref=w_own, dst_ref=w_held, send_sem=send_sem.at[8], recv_sem=recv_sem.at[8],
        device_id=bridge_id, device_id_type=MESH)
    w_over = pltpu.make_async_remote_copy(
        src_ref=w_held, dst_ref=w_far, send_sem=send_sem.at[9], recv_sem=recv_sem.at[0],
        device_id=tail_id, device_id_type=MESH)

    def await_barrier():
        pl.semaphore_wait(barrier, 1 + has_far.astype(jnp.int32) + tails.astype(jnp.int32))

    def send_basis(piece):
        @pl.when(jnp.logical_not(heads))
        def start_now():
            launch_far(p_sent[piece])

        p_sent[piece][1].start()

    def send_vector():
        @pl.when(jnp.logical_not(heads))
        def start_direct():
            launch_far(w_sent)

        @pl.when(heads)
        def start_up():
            w_up.start()

        w_sent[1].start()

    loads[0].wait()
    pc_own[...] = jnp.zeros_like(pc_own)
    for c in range(parts):
        for j in range(order):
            spot = at_row[c] + counts[c] * j
            pc_own[spot:spot + counts[c], :] = p_v[j, firsts[c]:firsts[c] + counts[c], :]

    @pl.when(jnp.logical_not(lazy))
    def meet():
        await_barrier()

        @pl.when(tails)
        def announce():
            pl.semaphore_signal(met_sem, inc=1, device_id=bridge_id, device_id_type=MESH)
            pl.semaphore_signal(met_sem, inc=1, device_id=far_id, device_id_type=MESH)

        send_basis(0)

    loads[1].wait()
    cell_row = lax.broadcasted_iota(jnp.int32, (cells, agg_count), 0)
    found = None
    for place in range(mem_v.shape[0]):
        hit = cell_row == mem_v[place:place + 1, :]
        found = hit if found is None else jnp.logical_or(found, hit)
    mt_s[...] = jnp.where(found, 1.0, 0.0).astype(BF16)
    eye = jnp.where(
        lax.broadcasted_iota(jnp.int32, (agg_count, agg_count), 0)
        == lax.broadcasted_iota(jnp.int32, (agg_count, agg_count), 1), 1.0, 0.0).astype(BF16)
    m_s[...] = dot_nt(eye, mt_s[...]).astype(BF16)

    loads[2].wait()
    v_pad[...] = jnp.zeros_like(v_pad)
    v_pad[0:order, :] = guess_v[...]
    high, low = halves(v_pad[...])
    v_cells = (dot_nn(high, m_s[...]) + dot_nn(low, m_s[...]))[0:order, :]
    w_own[...] = jnp.zeros_like(w_own)
    for j in range(order):
        w_own[j:j + 1, :] = jnp.sum(p_v[j] * v_cells, axis=0, keepdims=True)

    @pl.when(jnp.logical_not(lazy))
    def tell():
        send_vector()
        send_basis(1)

    loads[3].wait()
    loads[4].wait()
    idx_s[...] = jnp.zeros_like(idx_s)
    idx_s[0, 0:fine_rows, :] = col_v[...]
    is_odd = jnp.full((8, LANES), odd, jnp.int32)
    half = ghost_v.shape[0] * LANES // 2
    for t in range(tiles):
        at = slice(t * LANES, (t + 1) * LANES)
        col = idx_s[0, :, at]
        place = jnp.maximum(col - cells, 0)
        lane = jnp.bitwise_and(place, LANES - 1)
        part = jnp.right_shift(place, 7)
        cell = jnp.zeros((8, LANES), jnp.int32)
        for b in range(ghost_v.shape[0]):
            got = lane_gather(jnp.broadcast_to(ghost_v[b:b + 1, :], (8, LANES)), lane)
            cell = jnp.where(part == b, got, cell)
        own = col < cells
        after = jnp.where(col >= cells + half, 1, 0)
        same = after != is_odd
        idx_s[1, :, at] = jnp.where(own, col, -1)
        idx_s[2, :, at] = jnp.where(jnp.logical_and(jnp.logical_not(own), same), cell, -1)
        idx_s[3, :, at] = jnp.where(jnp.logical_or(own, same), -1, cell)
    ramp = lax.broadcasted_iota(jnp.int32, (256, cells), 0).astype(F32).astype(BF16)
    one = jnp.ones((256, cells), BF16)
    zero = jnp.zeros((256, cells), BF16)
    for group, hot in ((1, oh_own), (2, oh_near), (3, oh_far)):
        for k in range(rest):
            for block in range(cells // 256):
                line = (idx_s[group, k + 1:k + 2, :] - 256 * block).astype(F32).astype(BF16)
                hot[256 * block:256 * (block + 1), k * cells:(k + 1) * cells] = jnp.where(ramp == line, one, zero)

    def split_basis(source, c):
        high, low = halves(source[at_row[c]:at_row[c] + tall[c], :])
        phl_s[0:tall[c], 0:cells] = high
        phl_s[0:tall[c], cells:2 * cells] = low

    def basis_part(hot, c, k):
        hot_part = hot[:, k * cells:(k + 1) * cells]
        return dot_nn(phl_s[0:tall[c], :], jnp.concatenate([hot_part, hot_part], axis=0))

    def vector_part(hot, k):
        both = dot_nn(whl_s[...], hot[:, k * cells:(k + 1) * cells])
        return both[0:16, :] + both[16:32, :]

    def split_vector(source):
        high, low = halves(source[...])
        whl_s[0:16, :] = high
        whl_s[16:32, :] = low

    split_vector(w_own)
    for k in range(rest):
        wacc_s[:, k * cells:(k + 1) * cells] = vector_part(oh_own, k)
    for t in range(tiles):
        wg_s[pl.ds(t * LANES, 16, stride=8), :] = w_own[:, t * LANES:(t + 1) * LANES]

    for b in range(order // 2):
        loads[7 + b].wait()
    d_s[...] = jnp.zeros_like(d_s)
    for t in range(tiles):
        at = slice(t * LANES, (t + 1) * LANES)
        for r in range(order):
            total = None
            for j in range(order):
                term = a_v[r, j, 0:1, at] * p_v[j, :, at]
                total = term if total is None else total + term
            ap_s[r, 0:order, :] = total
        for i in range(order):
            total = None
            for r in range(order):
                term = p_v[r, i:i + 1, at] * ap_s[r, 0:order, :]
                total = term if total is None else total + term
            d_s[i, 0:order, at] = total
    deep = d_s.shape[1]
    high, low = halves(d_s[...].reshape(order * deep, cells))
    diagonal = (dot_nt(high, m_s[...]) + dot_nt(low, m_s[...])).reshape(order, deep, agg_count)
    wide = jnp.zeros((order, LANES - agg_count), F32)
    for i in range(order):
        for c in range(parts):
            line = jnp.concatenate([diagonal[i, firsts[c]:firsts[c] + counts[c], :], wide[0:counts[c]]], axis=1)
            op_s[pl.ds((op_row[c] + i * counts[c]) * 8, counts[c], stride=8), :] = line
    inverse = jnp.stack([op_s[pl.ds((op_row[c] + l) * 8, order, stride=counts[c] * 8), :][:, 0:agg_count]
                         for c in range(parts) for l in range(counts[c])])
    entry = lax.broadcasted_iota(jnp.int32, (order, agg_count), 0)
    row_at = lax.broadcasted_iota(jnp.int32, (order, 1, agg_count), 0)
    for pivot in range(order):
        line = inverse[pivot]
        scale = 1.0 / line[pivot:pivot + 1, :]
        line = jnp.where(entry == pivot, 1.0, line) * scale
        factor = inverse[:, pivot:pivot + 1, :]
        kept = jnp.where((entry == pivot)[None], 0.0, inverse)
        inverse = kept - factor * line[None]
        inverse = jnp.where(row_at == pivot, line[None], inverse)
    for i in range(order):
        small_s[16 * i + 32:16 * i + 32 + order, 0:agg_count] = inverse[i]

    loads[6].wait()
    z_s[...] = jnp.zeros_like(z_s)
    v_one[...] = jnp.zeros_like(v_one)

    def sweep():
        w_sent[1].wait_recv()
        split_vector(w_near)
        for k in range(rest):
            wacc_s[:, k * cells:(k + 1) * cells] += vector_part(oh_near, k)

        await_far(w_sent[0], w_far)
        split_vector(w_far)
        for k in range(rest):
            total = wacc_s[:, k * cells:(k + 1) * cells] + vector_part(oh_far, k)
            for t in range(tiles):
                wg_s[pl.ds(t * LANES + k + 1, 16, stride=8), :] = total[:, t * LANES:(t + 1) * LANES]

        for t in range(tiles):
            at = slice(t * LANES, (t + 1) * LANES)
            taken = [wg_s[t * LANES + j * 8:t * LANES + j * 8 + fine_rows, :] for j in range(order)]
            whole = None
            for r in range(order):
                total = None
                for j in range(order):
                    term = a_v[r, j, :, at] * taken[j]
                    total = term if total is None else total + term
                term = p_v[r, :, at] * jnp.sum(total, axis=0, keepdims=True)
                whole = term if whole is None else whole + term
            z_s[0:order, at] = whole

        high, low = halves(z_s[...])
        whl_s[0:16, :] = high
        whl_s[16:32, :] = low
        both = dot_nt(whl_s[...], m_s[...])
        residual = rhs_v[...] - (both[0:order, :] + both[16:16 + order, :])
        update = v_pad[0:order, :]
        for j in range(order):
            update = update + small_s[16 * j + 32:16 * j + 32 + order, 0:agg_count] * residual[j:j + 1, :]
        v_one[0:order, 0:agg_count] = update
        launch_far(v_sent)
        v_sent[1].start()

    def prepare():
        loads[5].wait()
        member = m_s[...]
        none = jnp.zeros_like(member)
        for k in range(rest):
            line = slot_v[k + 1:k + 2, :].astype(F32).astype(BF16)
            wide_line = jnp.broadcast_to(line, (agg_count, cells))
            for s in range(1, slots):
                picked = wide_line == jnp.full((agg_count, cells), s, BF16)
                rt_s[(s - 1) * agg_count:s * agg_count, k * cells:(k + 1) * cells] = jnp.where(picked, member, none)

        def q_step(step, carry):
            pair = step // tiles

            lanes = pl.ds(pl.multiple_of(lax.rem(step, tiles) * LANES, LANES), LANES)
            blocks = [[a_v[r, pair * 2 + jj, :, lanes] for r in range(order)] for jj in range(2)]
            for i in range(order):
                total = [None, None]
                for r in range(order):
                    basis = p_v[r, i:i + 1, lanes]
                    for jj in range(2):
                        term = basis * blocks[jj][r]
                        total[jj] = term if total[jj] is None else total[jj] + term
                for jj in range(2):
                    q_s[i, pair * 2 + jj, :, lanes] = total[jj]
            return carry

        lax.fori_loop(0, order // 2 * tiles, q_step, 0)

        @pl.when(lazy)
        def meet_late():
            await_barrier()
            send_vector()
            send_basis(0)
            send_basis(1)

        @pl.when(bridges)
        def hand_on():
            w_up.wait_recv()
            pl.semaphore_wait(met_sem, 1)
            w_over.start()

        for c in range(parts):
            split_basis(pc_own, c)
            for k in range(rest):
                acc_s[at_row[c]:at_row[c] + tall[c], k * cells:(k + 1) * cells] = basis_part(oh_own, c, k)
        for c in range(parts):
            for copies in p_sent:
                copies[1].wait_recv()
            split_basis(pc_near, c)
            for k in range(rest):
                acc_s[at_row[c]:at_row[c] + tall[c], k * cells:(k + 1) * cells] += basis_part(oh_near, c, k)

        @pl.when(heads)
        def start_late():
            pl.semaphore_wait(met_sem, 1)
            for copies in p_sent:
                copies[0].start()

    def turn(at, carry):
        @pl.when(jnp.logical_xor(at == 0, tails))
        def run_prepare():
            prepare()

        @pl.when(at == 0)
        def run_sweep():
            sweep()

        return carry

    lax.fori_loop(0, 2, turn, 0)

    def product_part(c):
        pairs_here = counts[c] // 2

        def product_step(step, carry):
            pair = step // tiles
            t = lax.rem(step, tiles)
            lanes = pl.ds(pl.multiple_of(t * LANES, LANES), LANES)
            base = t * span + pair * 16
            taken = [[g_s[pl.ds(pl.multiple_of(base + (j * counts[c] + ll) * 8, 8), fine_rows), :]
                      for j in range(order)] for ll in range(2)]
            for i in range(order):
                total = [None, None]
                for j in range(order):
                    left = q_s[i, j, :, lanes]
                    for ll in range(2):
                        term = left * taken[ll][j]
                        total[ll] = term if total[ll] is None else total[ll] + term
                for ll in range(2):
                    prod_s[pl.ds(pl.multiple_of(base + (i * counts[c] + ll) * 8, 8), fine_rows), :] = total[ll]
            return carry

        lax.fori_loop(0, pairs_here * tiles, product_step, 0)

    for c in range(parts):
        for copies, (a, b) in zip(p_sent, pieces):
            await_far(copies[0], pc_far.at[a:b])
        split_basis(pc_far, c)
        height = counts[c] * order
        for k in range(rest):
            total = acc_s[at_row[c]:at_row[c] + tall[c], k * cells:(k + 1) * cells] + basis_part(oh_far, c, k)
            for t in range(tiles):
                g_s[pl.ds(t * span + k + 1, height, stride=8), :] = total[0:height, t * LANES:(t + 1) * LANES]
        product_part(c)
        for k in range(rest):
            for t in range(tiles):
                high, low = halves(prod_s[pl.ds(t * span + k + 1, tall[c], stride=8), :])
                at = slice(k * cells + t * LANES, k * cells + (t + 1) * LANES)
                lhs_s[0:tall[c], at] = high
                lhs_s[tall[c]:2 * tall[c], at] = low
        both = dot_nt(lhs_s[0:2 * tall[c], :], rt_s[...])
        summed = both[0:height, :] + both[tall[c]:tall[c] + height, :]
        filler = jnp.zeros((height, LANES - agg_count), F32)
        for s in range(1, slots):
            part = summed[:, (s - 1) * agg_count:s * agg_count]
            op_s[pl.ds(op_row[c] * 8 + s, height, stride=8), :] = jnp.concatenate([part, filler], axis=1)

    v_sent[1].wait_recv()
    small_s[0:16, :] = jnp.concatenate([v_one[:, 0:agg_count], v_near[:, 0:agg_count]], axis=1)
    await_far(v_sent[0], v_far)
    small_s[16:32, :] = v_far[...]
    for copies in [v_sent] + p_sent:
        copies[1].wait_send()

        @pl.when(has_far)
        def drain():
            copies[0].wait_send()

    w_sent[1].wait_send()

    @pl.when(jnp.logical_and(has_far, jnp.logical_not(heads)))
    def drain_direct():
        w_sent[0].wait_send()

    @pl.when(heads)
    def drain_up():
        w_up.wait_send()

    @pl.when(bridges)
    def drain_over():
        w_over.wait_send()


def finish(n_fine, n_coarse, op_s, small_s, cc_v, rhs_v, op_ref, it_ref, cc_s):
    odd = lax.rem(lax.axis_index("coarse"), 2)
    is_odd = jnp.full((8, LANES), odd, jnp.int32)
    order, agg_count = rhs_v.shape
    slots = cc_v.shape[0]
    cc_s[...] = jnp.zeros_like(cc_s)
    cc_s[0:slots, 0:agg_count] = cc_v[...]
    column = cc_s[...]
    lane = jnp.bitwise_and(column, agg_count - 1)
    holder = column // agg_count
    is_near = holder == 2 - 2 * is_odd
    is_far = holder == 2 * is_odd
    first = lane + jnp.where(is_near, agg_count, 0)
    names = []
    for l in range(order):
        one_side = lane_gather(jnp.broadcast_to(small_s[l:l + 1, :], (8, LANES)), first)
        other = lane_gather(jnp.broadcast_to(small_s[16 + l:17 + l, :], (8, LANES)), lane)
        names.append(jnp.where(is_far, other, one_side)[0:slots, 0:agg_count])
    update = small_s[0:order, 0:agg_count]
    for i in range(order):
        total = None
        for l in range(order):
            row = (i * order + l) * 8
            block = op_s[row:row + slots, 0:agg_count]
            op_ref[i, l] = block
            term = block * names[l]
            total = term if total is None else total + term
        line = rhs_v[i:i + 1, :] - jnp.sum(total, axis=0, keepdims=True)
        update = update + small_s[16 * i + 32:16 * i + 32 + order, 0:agg_count] * line
    it_ref[...] = update


def body(n_fine, n_coarse, fine_blocks, fine_columns, coarse_slots, ghost_lists, tentative, members, coarse_columns,
         coarse_rhs, coarse_guess):
    fine_rows, order, _, cells = fine_blocks.shape
    slots, agg_count = coarse_columns.shape
    rest = fine_rows - 1
    ghosts = ghost_lists.reshape(-1, LANES)
    deep = -(-order * order // 16) * 16
    vm = pltpu.VMEM
    scratch = [
        vm((order, order, fine_rows, cells), F32), vm(fine_columns.shape, jnp.int32), vm(coarse_slots.shape, jnp.int32),
        vm(ghosts.shape, jnp.int32), vm(tentative.shape, F32), vm(members.shape, jnp.int32),
        vm(coarse_rhs.shape, F32), vm(coarse_guess.shape, F32),
        vm((16, agg_count), F32),
        vm((16, LANES), F32), vm((16, LANES), F32), vm((16, LANES), F32),
        vm((cells, agg_count), BF16), vm((agg_count, cells), BF16),
        vm((16, cells), F32), vm((16, cells), F32), vm((16, cells), F32), vm((16, cells), F32),
        vm((deep, cells), F32), vm((deep, cells), F32), vm((deep, cells), F32),
        vm((order, order, fine_rows, cells), F32), vm((order, 16, LANES), F32), vm((order, 16, cells), F32),
        vm((4, 8, cells), jnp.int32),
        vm((cells, rest * cells), BF16), vm((cells, rest * cells), BF16), vm((cells, rest * cells), BF16),
        vm((deep, 2 * cells), BF16), vm((32, cells), BF16), vm((16, rest * cells), F32),
        vm((cells // LANES * LANES, LANES), F32),
        vm((deep, rest * cells), F32),
        vm((cells // LANES * deep * 8, LANES), F32), vm((cells // LANES * deep * 8, LANES), F32),
        vm((16, cells), F32), vm((2 * deep, rest * cells), BF16), vm(((slots - 1) * agg_count, rest * cells), BF16),
        pltpu.SemaphoreType.DMA((7 + order // 2,)), pltpu.SemaphoreType.DMA((10,)), pltpu.SemaphoreType.DMA((9,)),
        pltpu.SemaphoreType.REGULAR,
    ]
    in_vmem = pl.BlockSpec(memory_space=pltpu.VMEM)
    padded, small = pl.pallas_call(
        functools.partial(kernel, n_fine, n_coarse),
        out_shape=(vm((order * order * 8, LANES), F32), vm((16 * order + 32, LANES), F32)),
        in_specs=[pl.BlockSpec(memory_space=pltpu.HBM)] * 8,
        out_specs=[in_vmem] * 2,
        scratch_shapes=scratch,
        compiler_params=pltpu.CompilerParams(collective_id=0, has_side_effects=True, vmem_limit_bytes=40 * 2**20),
    )(*[pltpu.with_memory_space_constraint(given, pltpu.HBM) for given in (
        jnp.transpose(fine_blocks, (1, 2, 0, 3)), fine_columns, coarse_slots, ghosts, tentative, members, coarse_rhs,
        coarse_guess)])
    op, iterate = pl.pallas_call(
        functools.partial(finish, n_fine, n_coarse),
        out_shape=(jax.ShapeDtypeStruct((order, order, slots, agg_count), F32),
                   jax.ShapeDtypeStruct((order, agg_count), F32)),
        in_specs=[in_vmem] * 4,
        out_specs=[in_vmem] * 2,
        scratch_shapes=[vm((8, LANES), jnp.int32)],
        compiler_params=pltpu.CompilerParams(vmem_limit_bytes=8 * 2**20),
    )(padded, small, coarse_columns, coarse_rhs)
    return jnp.transpose(op, (2, 0, 1, 3)), iterate


def solution(mesh):
    both = ("fine", "coarse")
    placed = (
        P(None, None, None, both), P(None, both), P(None, both), P(both), P(None, None, both), P(None, both),
        P(None, both), P(None, both), P(None, both),
    )
    return jax.shard_map(
        functools.partial(body, mesh.shape["fine"], mesh.shape["coarse"]),
        mesh=mesh,
        in_specs=placed,
        out_specs=(P(None, None, None, both), P(None, both)),
        check_vma=False,
    )
```

```python
import functools

import jax
import jax.numpy as jnp
from jax import lax
from jax.experimental import pallas as pl
from jax.experimental.pallas import tpu as pltpu
from jax.sharding import PartitionSpec as P

F32 = jnp.float32
BF16 = jnp.bfloat16
MESH = pl.DeviceIdType.MESH
LANES = 128


def lane_gather(table, index):
    return jnp.take_along_axis(table, index, axis=1, mode="promise_in_bounds")


def column_parts(order):
    return (0,), (order,)


def halves(value):
    high = value.astype(BF16)
    low = (value - high.astype(F32)).astype(BF16)
    return high, low


def dot_nn(left, right):
    return lax.dot_general(left, right, (((1,), (0,)), ((), ())), preferred_element_type=F32)


def dot_nt(left, right):
    return lax.dot_general(left, right, (((1,), (1,)), ((), ())), preferred_element_type=F32)


def kernel(
    n_fine, n_coarse,
    a_hbm, col_hbm, slot_hbm, ghost_hbm, p_hbm, mem_hbm, rhs_hbm, guess_hbm,
    op_s, small_s,
    a_v, col_v, slot_v, ghost_v, p_v, mem_v, rhs_v, guess_v,
    v_pad, v_one, v_near, v_far,
    mt_s, m_s, w_own, w_near, w_far, w_held, pc_own, pc_near, pc_far,
    q_s, ap_s, d_s, idx_s, oh_own, oh_near, oh_far,
    phl_s, whl_s, wacc_s, wg_s, acc_s, g_s, prod_s, z_s, lhs_s, rt_s,
    in_sem, send_sem, recv_sem, met_sem,
):
    n_all = n_fine * n_coarse
    me = lax.axis_index("fine") * n_coarse + lax.axis_index("coarse")
    odd = lax.rem(me, 2)
    near = me + 1 - 2 * odd
    far = lax.rem(me + n_all - 1 + 2 * odd, n_all)
    near_id = (near // n_coarse, lax.rem(near, n_coarse))
    far_id = (far // n_coarse, lax.rem(far, n_coarse))

    has_far = jnp.logical_and(jnp.logical_or(odd == 1, me > 0), jnp.logical_or(odd == 0, me < n_all - 1))
    lap = 8 * n_coarse
    heads = jnp.logical_and(lax.rem(me, lap) == 0, me > 0)
    tails = jnp.logical_and(lax.rem(me, lap) == lap - 1, me < n_all - 1)
    bridges = jnp.logical_and(lax.rem(me, lap) == n_coarse - 1, me < n_all - lap)
    lap_head = lax.rem((me // lap + 1) * lap, n_all)
    head_id = (lap_head // n_coarse, lax.rem(lap_head, n_coarse))
    lap_tail = (me // lap + 1) * lap - 1
    tail_id = (lap_tail // n_coarse, lax.rem(lap_tail, n_coarse))
    bridge = jnp.where(heads, me - lap, me // lap * lap) + n_coarse - 1
    bridge_id = (bridge // n_coarse, lax.rem(bridge, n_coarse))
    lazy = me == 1

    barrier = pltpu.get_barrier_semaphore()

    @pl.when(jnp.logical_and(has_far, jnp.logical_not(tails)))
    def greet():
        pl.semaphore_signal(barrier, inc=1, device_id=far_id, device_id_type=MESH)

    pl.semaphore_signal(barrier, inc=1, device_id=near_id, device_id_type=MESH)

    @pl.when(bridges)
    def greet_lap():
        pl.semaphore_signal(barrier, inc=1, device_id=tail_id, device_id_type=MESH)
        pl.semaphore_signal(barrier, inc=1, device_id=head_id, device_id_type=MESH)

    order, agg_count = rhs_v.shape
    slots = 1 + rt_s.shape[0] // agg_count
    fine_rows = a_v.shape[2]
    cells = p_v.shape[2]
    tiles = cells // LANES
    firsts, counts = column_parts(order)
    sent = [-(-count * order // 8) * 8 for count in counts]
    tall = [-(-count * order // 16) * 16 for count in counts]
    at_row = (0,)
    op_row = (0,)
    parts = len(counts)
    span = prod_s.shape[0] // tiles
    rest = fine_rows - 1

    pairs = [(p_hbm, p_v), (mem_hbm, mem_v), (guess_hbm, guess_v), (col_hbm, col_v), (ghost_hbm, ghost_v),
             (slot_hbm, slot_v), (rhs_hbm, rhs_v)]
    pairs += [(a_hbm.at[:, 2 * b:2 * b + 2], a_v.at[:, 2 * b:2 * b + 2]) for b in range(order // 2)]
    loads = [pltpu.make_async_copy(src, dst, in_sem.at[i]) for i, (src, dst) in enumerate(pairs)]
    for load in loads:
        load.start()

    def exchange(source, to_near, to_far, base):
        return [pltpu.make_async_remote_copy(
            src_ref=source, dst_ref=dst, send_sem=send_sem.at[base + at], recv_sem=recv_sem.at[base + at],
            device_id=ident, device_id_type=MESH)
            for at, (dst, ident) in enumerate(((to_far, far_id), (to_near, near_id)))]

    def launch_far(copies):
        @pl.when(has_far)
        def start_far():
            copies[0].start()

    def await_far(copy, landing):
        @pl.when(has_far)
        def take():
            copy.wait_recv()

        @pl.when(jnp.logical_not(has_far))
        def clear():
            landing[...] = jnp.zeros_like(landing)

    w_sent = exchange(w_own, w_near, w_far, 0)
    v_sent = exchange(v_one, v_near, v_far, 2)
    pieces = ((0, 48), (48, sent[0]))
    p_sent = [exchange(*(ref.at[a:b] for ref in (pc_own, pc_near, pc_far)), 4 + 2 * n)
              for n, (a, b) in enumerate(pieces)]
    w_up = pltpu.make_async_remote_copy(
        src_ref=w_own, dst_ref=w_held, send_sem=send_sem.at[8], recv_sem=recv_sem.at[8],
        device_id=bridge_id, device_id_type=MESH)
    w_over = pltpu.make_async_remote_copy(
        src_ref=w_held, dst_ref=w_far, send_sem=send_sem.at[9], recv_sem=recv_sem.at[0],
        device_id=tail_id, device_id_type=MESH)

    def await_barrier():
        pl.semaphore_wait(barrier, 1 + has_far.astype(jnp.int32) + tails.astype(jnp.int32))

    def send_basis(piece):
        @pl.when(jnp.logical_not(heads))
        def start_now():
            launch_far(p_sent[piece])

        p_sent[piece][1].start()

    def send_vector():
        @pl.when(jnp.logical_not(heads))
        def start_direct():
            launch_far(w_sent)

        @pl.when(heads)
        def start_up():
            w_up.start()

        w_sent[1].start()

    @pl.when(tails)
    def announce():
        await_barrier()
        pl.semaphore_signal(met_sem, inc=1, device_id=bridge_id, device_id_type=MESH)
        pl.semaphore_signal(met_sem, inc=1, device_id=far_id, device_id_type=MESH)

    loads[0].wait()
    pc_own[...] = jnp.zeros_like(pc_own)
    for c in range(parts):
        for j in range(order):
            spot = at_row[c] + counts[c] * j
            pc_own[spot:spot + counts[c], :] = p_v[j, firsts[c]:firsts[c] + counts[c], :]

    @pl.when(jnp.logical_not(lazy))
    def meet():
        @pl.when(jnp.logical_not(tails))
        def meet_now():
            await_barrier()

        send_basis(0)

    loads[1].wait()
    cell_row = lax.broadcasted_iota(jnp.int32, (cells, agg_count), 0)
    found = None
    for place in range(mem_v.shape[0]):
        hit = cell_row == mem_v[place:place + 1, :]
        found = hit if found is None else jnp.logical_or(found, hit)
    mt_s[...] = jnp.where(found, 1.0, 0.0).astype(BF16)

    loads[2].wait()
    v_pad[...] = jnp.zeros_like(v_pad)
    v_pad[0:order, :] = guess_v[...]
    high, low = halves(v_pad[...])
    whl_s[0:16, 0:agg_count] = high
    whl_s[16:32, 0:agg_count] = low
    both = dot_nt(whl_s[:, 0:agg_count], mt_s[...])
    v_cells = both[0:order, :] + both[16:16 + order, :]
    w_own[...] = jnp.zeros_like(w_own)
    for j in range(order):
        w_own[j:j + 1, :] = jnp.sum(p_v[j] * v_cells, axis=0, keepdims=True)

    @pl.when(jnp.logical_not(lazy))
    def tell():
        send_vector()
        send_basis(1)

    eye = jnp.where(
        lax.broadcasted_iota(jnp.int32, (agg_count, agg_count), 0)
        == lax.broadcasted_iota(jnp.int32, (agg_count, agg_count), 1), 1.0, 0.0).astype(BF16)
    m_s[...] = dot_nt(eye, mt_s[...]).astype(BF16)

    loads[3].wait()
    loads[4].wait()
    idx_s[...] = jnp.zeros_like(idx_s)
    idx_s[0, 0:fine_rows, :] = col_v[...]
    is_odd = jnp.full((8, LANES), odd, jnp.int32)
    half = ghost_v.shape[0] * LANES // 2
    for t in range(tiles):
        at = slice(t * LANES, (t + 1) * LANES)
        col = idx_s[0, :, at]
        place = jnp.maximum(col - cells, 0)
        lane = jnp.bitwise_and(place, LANES - 1)
        part = jnp.right_shift(place, 7)
        cell = jnp.zeros((8, LANES), jnp.int32)
        for b in range(ghost_v.shape[0]):
            got = lane_gather(jnp.broadcast_to(ghost_v[b:b + 1, :], (8, LANES)), lane)
            cell = jnp.where(part == b, got, cell)
        own = col < cells
        after = jnp.where(col >= cells + half, 1, 0)
        same = after != is_odd
        idx_s[1, :, at] = jnp.where(own, col, -1)
        idx_s[2, :, at] = jnp.where(jnp.logical_and(jnp.logical_not(own), same), cell, -1)
        idx_s[3, :, at] = jnp.where(jnp.logical_or(own, same), -1, cell)
    ramp = lax.broadcasted_iota(jnp.int32, (256, cells), 0).astype(F32).astype(BF16)
    one = jnp.ones((256, cells), BF16)
    zero = jnp.zeros((256, cells), BF16)
    for group, hot in ((1, oh_own), (2, oh_near), (3, oh_far)):
        for k in range(rest):
            for block in range(cells // 256):
                line = (idx_s[group, k + 1:k + 2, :] - 256 * block).astype(F32).astype(BF16)
                hot[256 * block:256 * (block + 1), k * cells:(k + 1) * cells] = jnp.where(ramp == line, one, zero)

    def split_basis(source, c):
        high, low = halves(source[at_row[c]:at_row[c] + tall[c], :])
        phl_s[0:tall[c], 0:cells] = high
        phl_s[0:tall[c], cells:2 * cells] = low

    def basis_part(hot, c, k):
        hot_part = hot[:, k * cells:(k + 1) * cells]
        return dot_nn(phl_s[0:tall[c], :], jnp.concatenate([hot_part, hot_part], axis=0))

    def vector_part(hot, k):
        both = dot_nn(whl_s[...], hot[:, k * cells:(k + 1) * cells])
        return both[0:16, :] + both[16:32, :]

    def split_vector(source):
        high, low = halves(source[...])
        whl_s[0:16, :] = high
        whl_s[16:32, :] = low

    split_vector(w_own)
    for k in range(rest):
        wacc_s[:, k * cells:(k + 1) * cells] = vector_part(oh_own, k)
    for t in range(tiles):
        wg_s[pl.ds(t * LANES, 16, stride=8), :] = w_own[:, t * LANES:(t + 1) * LANES]

    for b in range(order // 2):
        loads[7 + b].wait()
    d_s[...] = jnp.zeros_like(d_s)
    for t in range(tiles):
        at = slice(t * LANES, (t + 1) * LANES)
        for r in range(order):
            total = None
            for j in range(order):
                term = a_v[r, j, 0:1, at] * p_v[j, :, at]
                total = term if total is None else total + term
            ap_s[r, 0:order, :] = total
        for i in range(order):
            total = None
            for r in range(order):
                term = p_v[r, i:i + 1, at] * ap_s[r, 0:order, :]
                total = term if total is None else total + term
            d_s[i, 0:order, at] = total
    deep = d_s.shape[1]
    high, low = halves(d_s[...].reshape(order * deep, cells))
    diagonal = (dot_nt(high, m_s[...]) + dot_nt(low, m_s[...])).reshape(order, deep, agg_count)
    wide = jnp.zeros((order, LANES - agg_count), F32)
    for i in range(order):
        for c in range(parts):
            line = jnp.concatenate([diagonal[i, firsts[c]:firsts[c] + counts[c], :], wide[0:counts[c]]], axis=1)
            op_s[pl.ds((op_row[c] + i * counts[c]) * 8, counts[c], stride=8), :] = line
    inverse = jnp.stack([op_s[pl.ds((op_row[c] + l) * 8, order, stride=counts[c] * 8), :][:, 0:agg_count]
                         for c in range(parts) for l in range(counts[c])])
    entry = lax.broadcasted_iota(jnp.int32, (order, agg_count), 0)
    row_at = lax.broadcasted_iota(jnp.int32, (order, 1, agg_count), 0)
    for pivot in range(order):
        line = inverse[pivot]
        scale = 1.0 / line[pivot:pivot + 1, :]
        line = jnp.where(entry == pivot, 1.0, line) * scale
        factor = inverse[:, pivot:pivot + 1, :]
        kept = jnp.where((entry == pivot)[None], 0.0, inverse)
        inverse = kept - factor * line[None]
        inverse = jnp.where(row_at == pivot, line[None], inverse)
    for i in range(order):
        small_s[16 * i + 32:16 * i + 32 + order, 0:agg_count] = inverse[i]

    loads[6].wait()
    z_s[...] = jnp.zeros_like(z_s)
    v_one[...] = jnp.zeros_like(v_one)

    def sweep():
        w_sent[1].wait_recv()
        split_vector(w_near)
        for k in range(rest):
            wacc_s[:, k * cells:(k + 1) * cells] += vector_part(oh_near, k)

        await_far(w_sent[0], w_far)
        split_vector(w_far)
        for k in range(rest):
            total = wacc_s[:, k * cells:(k + 1) * cells] + vector_part(oh_far, k)
            for t in range(tiles):
                wg_s[pl.ds(t * LANES + k + 1, 16, stride=8), :] = total[:, t * LANES:(t + 1) * LANES]

        for t in range(tiles):
            at = slice(t * LANES, (t + 1) * LANES)
            taken = [wg_s[t * LANES + j * 8:t * LANES + j * 8 + fine_rows, :] for j in range(order)]
            whole = None
            for r in range(order):
                total = None
                for j in range(order):
                    term = a_v[r, j, :, at] * taken[j]
                    total = term if total is None else total + term
                term = p_v[r, :, at] * jnp.sum(total, axis=0, keepdims=True)
                whole = term if whole is None else whole + term
            z_s[0:order, at] = whole

        high, low = halves(z_s[...])
        whl_s[0:16, :] = high
        whl_s[16:32, :] = low
        both = dot_nt(whl_s[...], m_s[...])
        residual = rhs_v[...] - (both[0:order, :] + both[16:16 + order, :])
        update = v_pad[0:order, :]
        for j in range(order):
            update = update + small_s[16 * j + 32:16 * j + 32 + order, 0:agg_count] * residual[j:j + 1, :]
        v_one[0:order, 0:agg_count] = update
        launch_far(v_sent)
        v_sent[1].start()

    def prepare():
        loads[5].wait()
        member = m_s[...]
        none = jnp.zeros_like(member)
        for k in range(rest):
            line = slot_v[k + 1:k + 2, :].astype(F32).astype(BF16)
            wide_line = jnp.broadcast_to(line, (agg_count, cells))
            for s in range(1, slots):
                picked = wide_line == jnp.full((agg_count, cells), s, BF16)
                rt_s[(s - 1) * agg_count:s * agg_count, k * cells:(k + 1) * cells] = jnp.where(picked, member, none)

        def q_step(step, carry):
            pair = step // tiles

            lanes = pl.ds(pl.multiple_of(lax.rem(step, tiles) * LANES, LANES), LANES)
            blocks = [[a_v[r, pair * 2 + jj, :, lanes] for r in range(order)] for jj in range(2)]
            for i in range(order):
                total = [None, None]
                for r in range(order):
                    basis = p_v[r, i:i + 1, lanes]
                    for jj in range(2):
                        term = basis * blocks[jj][r]
                        total[jj] = term if total[jj] is None else total[jj] + term
                for jj in range(2):
                    q_s[i, pair * 2 + jj, :, lanes] = total[jj]
            return carry

        lax.fori_loop(0, order // 2 * tiles, q_step, 0)

        @pl.when(lazy)
        def meet_late():
            await_barrier()
            send_vector()
            send_basis(0)
            send_basis(1)

        @pl.when(bridges)
        def hand_on():
            w_up.wait_recv()
            pl.semaphore_wait(met_sem, 1)
            w_over.start()

        for c in range(parts):
            split_basis(pc_own, c)
            for k in range(rest):
                acc_s[at_row[c]:at_row[c] + tall[c], k * cells:(k + 1) * cells] = basis_part(oh_own, c, k)
        for c in range(parts):
            for copies in p_sent:
                copies[1].wait_recv()
            split_basis(pc_near, c)
            for k in range(rest):
                acc_s[at_row[c]:at_row[c] + tall[c], k * cells:(k + 1) * cells] += basis_part(oh_near, c, k)

        @pl.when(heads)
        def start_late():
            pl.semaphore_wait(met_sem, 1)
            for copies in p_sent:
                copies[0].start()

    def turn(at, carry):
        @pl.when(jnp.logical_xor(at == 0, tails))
        def run_prepare():
            prepare()

        @pl.when(at == 0)
        def run_sweep():
            sweep()

        return carry

    lax.fori_loop(0, 2, turn, 0)

    def product_part(c):
        pairs_here = counts[c] // 2

        def product_step(step, carry):
            product_tile(step // (tiles // 2), lax.rem(step, tiles // 2) * 2)
            product_tile(step // (tiles // 2), lax.rem(step, tiles // 2) * 2 + 1)
            return carry

        def product_tile(pair, t):
            lanes = pl.ds(pl.multiple_of(t * LANES, LANES), LANES)
            base = t * span + pair * 16
            taken = [[g_s[pl.ds(pl.multiple_of(base + (j * counts[c] + ll) * 8, 8), fine_rows), :]
                      for j in range(order)] for ll in range(2)]
            for i in range(order):
                total = [None, None]
                for j in range(order):
                    left = q_s[i, j, :, lanes]
                    for ll in range(2):
                        term = left * taken[ll][j]
                        total[ll] = term if total[ll] is None else total[ll] + term
                for ll in range(2):
                    prod_s[pl.ds(pl.multiple_of(base + (i * counts[c] + ll) * 8, 8), fine_rows), :] = total[ll]
        lax.fori_loop(0, pairs_here * tiles // 2, product_step, 0)

    for c in range(parts):
        for copies, (a, b) in zip(p_sent, pieces):
            await_far(copies[0], pc_far.at[a:b])
        split_basis(pc_far, c)
        height = counts[c] * order
        for k in range(rest):
            total = acc_s[at_row[c]:at_row[c] + tall[c], k * cells:(k + 1) * cells] + basis_part(oh_far, c, k)
            for t in range(tiles):
                g_s[pl.ds(t * span + k + 1, height, stride=8), :] = total[0:height, t * LANES:(t + 1) * LANES]
        product_part(c)
        for k in range(rest):
            for t in range(tiles):
                high, low = halves(prod_s[pl.ds(t * span + k + 1, tall[c], stride=8), :])
                at = slice(k * cells + t * LANES, k * cells + (t + 1) * LANES)
                lhs_s[0:tall[c], at] = high
                lhs_s[tall[c]:2 * tall[c], at] = low
        both = dot_nt(lhs_s[0:2 * tall[c], :], rt_s[...])
        summed = both[0:height, :] + both[tall[c]:tall[c] + height, :]
        filler = jnp.zeros((height, LANES - agg_count), F32)
        for s in range(1, slots):
            part = summed[:, (s - 1) * agg_count:s * agg_count]
            op_s[pl.ds(op_row[c] * 8 + s, height, stride=8), :] = jnp.concatenate([part, filler], axis=1)

    v_sent[1].wait_recv()
    small_s[0:16, :] = jnp.concatenate([v_one[:, 0:agg_count], v_near[:, 0:agg_count]], axis=1)
    await_far(v_sent[0], v_far)
    small_s[16:32, :] = v_far[...]
    for copies in [v_sent] + p_sent:
        copies[1].wait_send()

        @pl.when(has_far)
        def drain():
            copies[0].wait_send()

    w_sent[1].wait_send()

    @pl.when(jnp.logical_and(has_far, jnp.logical_not(heads)))
    def drain_direct():
        w_sent[0].wait_send()

    @pl.when(heads)
    def drain_up():
        w_up.wait_send()

    @pl.when(bridges)
    def drain_over():
        w_over.wait_send()


def finish(n_fine, n_coarse, op_s, small_s, cc_v, rhs_v, op_ref, it_ref, cc_s):
    odd = lax.rem(lax.axis_index("coarse"), 2)
    is_odd = jnp.full((8, LANES), odd, jnp.int32)
    order, agg_count = rhs_v.shape
    slots = cc_v.shape[0]
    cc_s[...] = jnp.zeros_like(cc_s)
    cc_s[0:slots, 0:agg_count] = cc_v[...]
    column = cc_s[...]
    lane = jnp.bitwise_and(column, agg_count - 1)
    holder = column // agg_count
    is_near = holder == 2 - 2 * is_odd
    is_far = holder == 2 * is_odd
    first = lane + jnp.where(is_near, agg_count, 0)
    names = []
    for l in range(order):
        one_side = lane_gather(jnp.broadcast_to(small_s[l:l + 1, :], (8, LANES)), first)
        other = lane_gather(jnp.broadcast_to(small_s[16 + l:17 + l, :], (8, LANES)), lane)
        names.append(jnp.where(is_far, other, one_side)[0:slots, 0:agg_count])
    update = small_s[0:order, 0:agg_count]
    for i in range(order):
        total = None
        for l in range(order):
            row = (i * order + l) * 8
            block = op_s[row:row + slots, 0:agg_count]
            op_ref[i, l] = block
            term = block * names[l]
            total = term if total is None else total + term
        line = rhs_v[i:i + 1, :] - jnp.sum(total, axis=0, keepdims=True)
        update = update + small_s[16 * i + 32:16 * i + 32 + order, 0:agg_count] * line
    it_ref[...] = update


def body(n_fine, n_coarse, fine_blocks, fine_columns, coarse_slots, ghost_lists, tentative, members, coarse_columns,
         coarse_rhs, coarse_guess):
    fine_rows, order, _, cells = fine_blocks.shape
    slots, agg_count = coarse_columns.shape
    rest = fine_rows - 1
    ghosts = ghost_lists.reshape(-1, LANES)
    deep = -(-order * order // 16) * 16
    vm = pltpu.VMEM
    scratch = [
        vm((order, order, fine_rows, cells), F32), vm(fine_columns.shape, jnp.int32), vm(coarse_slots.shape, jnp.int32),
        vm(ghosts.shape, jnp.int32), vm(tentative.shape, F32), vm(members.shape, jnp.int32),
        vm(coarse_rhs.shape, F32), vm(coarse_guess.shape, F32),
        vm((16, agg_count), F32),
        vm((16, LANES), F32), vm((16, LANES), F32), vm((16, LANES), F32),
        vm((cells, agg_count), BF16), vm((agg_count, cells), BF16),
        vm((16, cells), F32), vm((16, cells), F32), vm((16, cells), F32), vm((16, cells), F32),
        vm((deep, cells), F32), vm((deep, cells), F32), vm((deep, cells), F32),
        vm((order, order, fine_rows, cells), F32), vm((order, 16, LANES), F32), vm((order, 16, cells), F32),
        vm((4, 8, cells), jnp.int32),
        vm((cells, rest * cells), BF16), vm((cells, rest * cells), BF16), vm((cells, rest * cells), BF16),
        vm((deep, 2 * cells), BF16), vm((32, cells), BF16), vm((16, rest * cells), F32),
        vm((cells // LANES * LANES, LANES), F32),
        vm((deep, rest * cells), F32),
        vm((cells // LANES * deep * 8, LANES), F32), vm((cells // LANES * deep * 8, LANES), F32),
        vm((16, cells), F32), vm((2 * deep, rest * cells), BF16), vm(((slots - 1) * agg_count, rest * cells), BF16),
        pltpu.SemaphoreType.DMA((7 + order // 2,)), pltpu.SemaphoreType.DMA((10,)), pltpu.SemaphoreType.DMA((9,)),
        pltpu.SemaphoreType.REGULAR,
    ]
    in_vmem = pl.BlockSpec(memory_space=pltpu.VMEM)
    padded, small = pl.pallas_call(
        functools.partial(kernel, n_fine, n_coarse),
        out_shape=(vm((order * order * 8, LANES), F32), vm((16 * order + 32, LANES), F32)),
        in_specs=[pl.BlockSpec(memory_space=pltpu.HBM)] * 8,
        out_specs=[in_vmem] * 2,
        scratch_shapes=scratch,
        compiler_params=pltpu.CompilerParams(collective_id=0, has_side_effects=True, vmem_limit_bytes=40 * 2**20),
    )(*[pltpu.with_memory_space_constraint(given, pltpu.HBM) for given in (
        jnp.transpose(fine_blocks, (1, 2, 0, 3)), fine_columns, coarse_slots, ghosts, tentative, members, coarse_rhs,
        coarse_guess)])
    op, iterate = pl.pallas_call(
        functools.partial(finish, n_fine, n_coarse),
        out_shape=(jax.ShapeDtypeStruct((order, order, slots, agg_count), F32),
                   jax.ShapeDtypeStruct((order, agg_count), F32)),
        in_specs=[in_vmem] * 4,
        out_specs=[in_vmem] * 2,
        scratch_shapes=[vm((8, LANES), jnp.int32)],
        compiler_params=pltpu.CompilerParams(vmem_limit_bytes=8 * 2**20),
    )(padded, small, coarse_columns, coarse_rhs)
    return jnp.transpose(op, (2, 0, 1, 3)), iterate


def solution(mesh):
    both = ("fine", "coarse")
    placed = (
        P(None, None, None, both), P(None, both), P(None, both), P(both), P(None, None, both), P(None, both),
        P(None, both), P(None, both), P(None, both),
    )
    return jax.shard_map(
        functools.partial(body, mesh.shape["fine"], mesh.shape["coarse"]),
        mesh=mesh,
        in_specs=placed,
        out_specs=(P(None, None, None, both), P(None, both)),
        check_vma=False,
    )
```

```python
import functools

import jax
import jax.numpy as jnp
from jax import lax
from jax.experimental import pallas as pl
from jax.experimental.pallas import tpu as pltpu
from jax.sharding import PartitionSpec as P

F32 = jnp.float32
BF16 = jnp.bfloat16
MESH = pl.DeviceIdType.MESH
LANES = 128


def lane_gather(table, index):
    return jnp.take_along_axis(table, index, axis=1, mode="promise_in_bounds")


def column_parts(order):
    return (0,), (order,)


def halves(value):
    high = value.astype(BF16)
    low = (value - high.astype(F32)).astype(BF16)
    return high, low


def dot_nn(left, right):
    return lax.dot_general(left, right, (((1,), (0,)), ((), ())), preferred_element_type=F32)


def dot_nt(left, right):
    return lax.dot_general(left, right, (((1,), (1,)), ((), ())), preferred_element_type=F32)


def kernel(
    n_fine, n_coarse,
    a_hbm, col_hbm, slot_hbm, ghost_hbm, p_hbm, mem_hbm, rhs_hbm, guess_hbm,
    op_s, small_s,
    a_v, col_v, slot_v, ghost_v, p_v, mem_v, rhs_v, guess_v,
    v_pad, v_one, v_near, v_far,
    mt_s, m_s, w_own, w_near, w_far, w_held, pc_own, pc_near, pc_far,
    q_s, ap_s, d_s, idx_s, oh_own, oh_near, oh_far,
    phl_s, whl_s, wacc_s, wg_s, acc_s, g_s, prod_s, z_s, lhs_s, rt_s,
    in_sem, send_sem, recv_sem, met_sem,
):
    n_all = n_fine * n_coarse
    me = lax.axis_index("fine") * n_coarse + lax.axis_index("coarse")
    odd = lax.rem(me, 2)
    near = me + 1 - 2 * odd
    far = lax.rem(me + n_all - 1 + 2 * odd, n_all)
    near_id = (near // n_coarse, lax.rem(near, n_coarse))
    far_id = (far // n_coarse, lax.rem(far, n_coarse))

    has_far = jnp.logical_and(jnp.logical_or(odd == 1, me > 0), jnp.logical_or(odd == 0, me < n_all - 1))
    lap = 8 * n_coarse
    heads = jnp.logical_and(lax.rem(me, lap) == 0, me > 0)
    tails = jnp.logical_and(lax.rem(me, lap) == lap - 1, me < n_all - 1)
    bridges = jnp.logical_and(lax.rem(me, lap) == n_coarse - 1, me < n_all - lap)
    lap_head = lax.rem((me // lap + 1) * lap, n_all)
    head_id = (lap_head // n_coarse, lax.rem(lap_head, n_coarse))
    lap_tail = (me // lap + 1) * lap - 1
    tail_id = (lap_tail // n_coarse, lax.rem(lap_tail, n_coarse))
    bridge = jnp.where(heads, me - lap, me // lap * lap) + n_coarse - 1
    bridge_id = (bridge // n_coarse, lax.rem(bridge, n_coarse))
    lazy = me == 1

    barrier = pltpu.get_barrier_semaphore()

    @pl.when(jnp.logical_and(has_far, jnp.logical_not(tails)))
    def greet():
        pl.semaphore_signal(barrier, inc=1, device_id=far_id, device_id_type=MESH)

    pl.semaphore_signal(barrier, inc=1, device_id=near_id, device_id_type=MESH)

    @pl.when(bridges)
    def greet_lap():
        pl.semaphore_signal(barrier, inc=1, device_id=tail_id, device_id_type=MESH)
        pl.semaphore_signal(barrier, inc=1, device_id=head_id, device_id_type=MESH)

    order, agg_count = rhs_v.shape
    slots = 1 + rt_s.shape[0] // agg_count
    fine_rows = a_v.shape[2]
    cells = p_v.shape[2]
    tiles = cells // LANES
    firsts, counts = column_parts(order)
    sent = [-(-count * order // 8) * 8 for count in counts]
    tall = [-(-count * order // 16) * 16 for count in counts]
    at_row = (0,)
    op_row = (0,)
    parts = len(counts)
    span = prod_s.shape[0] // tiles
    rest = fine_rows - 1

    pairs = [(p_hbm, p_v), (mem_hbm, mem_v), (guess_hbm, guess_v), (col_hbm, col_v), (ghost_hbm, ghost_v),
             (slot_hbm, slot_v), (rhs_hbm, rhs_v)]
    pairs += [(a_hbm.at[:, 2 * b:2 * b + 2], a_v.at[:, 2 * b:2 * b + 2]) for b in range(order // 2)]
    loads = [pltpu.make_async_copy(src, dst, in_sem.at[i]) for i, (src, dst) in enumerate(pairs)]
    for load in loads:
        load.start()

    def exchange(source, to_near, to_far, base):
        return [pltpu.make_async_remote_copy(
            src_ref=source, dst_ref=dst, send_sem=send_sem.at[base + at], recv_sem=recv_sem.at[base + at],
            device_id=ident, device_id_type=MESH)
            for at, (dst, ident) in enumerate(((to_far, far_id), (to_near, near_id)))]

    def launch_far(copies):
        @pl.when(has_far)
        def start_far():
            copies[0].start()

    def await_far(copy, landing):
        @pl.when(has_far)
        def take():
            copy.wait_recv()

        @pl.when(jnp.logical_not(has_far))
        def clear():
            landing[...] = jnp.zeros_like(landing)

    w_sent = exchange(w_own, w_near, w_far, 0)
    v_sent = exchange(v_one, v_near, v_far, 2)
    pieces = ((0, 48), (48, sent[0]))
    p_sent = [exchange(*(ref.at[a:b] for ref in (pc_own, pc_near, pc_far)), 4 + 2 * n)
              for n, (a, b) in enumerate(pieces)]
    w_up = pltpu.make_async_remote_copy(
        src_ref=w_own, dst_ref=w_held, send_sem=send_sem.at[8], recv_sem=recv_sem.at[8],
        device_id=bridge_id, device_id_type=MESH)
    w_over = pltpu.make_async_remote_copy(
        src_ref=w_held, dst_ref=w_far, send_sem=send_sem.at[9], recv_sem=recv_sem.at[0],
        device_id=tail_id, device_id_type=MESH)

    def await_barrier():
        pl.semaphore_wait(barrier, 1 + has_far.astype(jnp.int32) + tails.astype(jnp.int32))

    def send_basis(piece):
        @pl.when(jnp.logical_not(heads))
        def start_now():
            launch_far(p_sent[piece])

        p_sent[piece][1].start()

    def send_vector():
        @pl.when(jnp.logical_not(heads))
        def start_direct():
            launch_far(w_sent)

        @pl.when(heads)
        def start_up():
            w_up.start()

        w_sent[1].start()

    @pl.when(tails)
    def announce():
        await_barrier()
        pl.semaphore_signal(met_sem, inc=1, device_id=bridge_id, device_id_type=MESH)
        pl.semaphore_signal(met_sem, inc=1, device_id=far_id, device_id_type=MESH)

    loads[0].wait()
    pc_own[...] = jnp.zeros_like(pc_own)
    for c in range(parts):
        for j in range(order):
            spot = at_row[c] + counts[c] * j
            pc_own[spot:spot + counts[c], :] = p_v[j, firsts[c]:firsts[c] + counts[c], :]

    @pl.when(jnp.logical_not(lazy))
    def meet():
        @pl.when(jnp.logical_not(tails))
        def meet_now():
            await_barrier()

        send_basis(0)

    loads[1].wait()
    cell_row = lax.broadcasted_iota(jnp.int32, (cells, agg_count), 0)
    found = None
    for place in range(mem_v.shape[0]):
        hit = cell_row == mem_v[place:place + 1, :]
        found = hit if found is None else jnp.logical_or(found, hit)
    mt_s[...] = jnp.where(found, 1.0, 0.0).astype(BF16)

    loads[2].wait()
    v_pad[...] = jnp.zeros_like(v_pad)
    v_pad[0:order, :] = guess_v[...]
    high, low = halves(v_pad[...])
    whl_s[0:16, 0:agg_count] = high
    whl_s[16:32, 0:agg_count] = low
    both = dot_nt(whl_s[:, 0:agg_count], mt_s[...])
    v_cells = both[0:order, :] + both[16:16 + order, :]
    w_own[...] = jnp.zeros_like(w_own)
    for j in range(order):
        w_own[j:j + 1, :] = jnp.sum(p_v[j] * v_cells, axis=0, keepdims=True)

    @pl.when(jnp.logical_not(lazy))
    def tell():
        send_vector()
        send_basis(1)

    eye = jnp.where(
        lax.broadcasted_iota(jnp.int32, (agg_count, agg_count), 0)
        == lax.broadcasted_iota(jnp.int32, (agg_count, agg_count), 1), 1.0, 0.0).astype(BF16)
    m_s[...] = dot_nt(eye, mt_s[...]).astype(BF16)

    loads[3].wait()
    loads[4].wait()
    idx_s[...] = jnp.zeros_like(idx_s)
    idx_s[0, 0:fine_rows, :] = col_v[...]
    is_odd = jnp.full((8, LANES), odd, jnp.int32)
    half = ghost_v.shape[0] * LANES // 2
    for t in range(tiles):
        at = slice(t * LANES, (t + 1) * LANES)
        col = idx_s[0, :, at]
        place = jnp.maximum(col - cells, 0)
        lane = jnp.bitwise_and(place, LANES - 1)
        part = jnp.right_shift(place, 7)
        cell = jnp.zeros((8, LANES), jnp.int32)
        for b in range(ghost_v.shape[0]):
            got = lane_gather(jnp.broadcast_to(ghost_v[b:b + 1, :], (8, LANES)), lane)
            cell = jnp.where(part == b, got, cell)
        own = col < cells
        after = jnp.where(col >= cells + half, 1, 0)
        same = after != is_odd
        idx_s[1, :, at] = jnp.where(own, col, -1)
        idx_s[2, :, at] = jnp.where(jnp.logical_and(jnp.logical_not(own), same), cell, -1)
        idx_s[3, :, at] = jnp.where(jnp.logical_or(own, same), -1, cell)
    ramp = lax.broadcasted_iota(jnp.int32, (256, cells), 0).astype(F32).astype(BF16)
    one = jnp.ones((256, cells), BF16)
    zero = jnp.zeros((256, cells), BF16)
    for group, hot in ((1, oh_own), (2, oh_near), (3, oh_far)):
        for k in range(rest):
            for block in range(cells // 256):
                line = (idx_s[group, k + 1:k + 2, :] - 256 * block).astype(F32).astype(BF16)
                hot[256 * block:256 * (block + 1), k * cells:(k + 1) * cells] = jnp.where(ramp == line, one, zero)

    def split_basis(source, c):
        high, low = halves(source[at_row[c]:at_row[c] + tall[c], :])
        phl_s[0:tall[c], 0:cells] = high
        phl_s[0:tall[c], cells:2 * cells] = low

    def basis_part(hot, c, k):
        hot_part = hot[:, k * cells:(k + 1) * cells]
        return dot_nn(phl_s[0:tall[c], :], jnp.concatenate([hot_part, hot_part], axis=0))

    def vector_part(hot, k):
        both = dot_nn(whl_s[...], hot[:, k * cells:(k + 1) * cells])
        return both[0:16, :] + both[16:32, :]

    def split_vector(source):
        high, low = halves(source[...])
        whl_s[0:16, :] = high
        whl_s[16:32, :] = low

    split_vector(w_own)
    for k in range(rest):
        wacc_s[:, k * cells:(k + 1) * cells] = vector_part(oh_own, k)
    for t in range(tiles):
        wg_s[pl.ds(t * LANES, 16, stride=8), :] = w_own[:, t * LANES:(t + 1) * LANES]

    for b in range(order // 2):
        loads[7 + b].wait()
    d_s[...] = jnp.zeros_like(d_s)
    for t in range(tiles):
        at = slice(t * LANES, (t + 1) * LANES)
        for r in range(order):
            total = None
            for j in range(order):
                term = a_v[r, j, 0:1, at] * p_v[j, :, at]
                total = term if total is None else total + term
            ap_s[r, 0:order, :] = total
        for i in range(order):
            total = None
            for r in range(order):
                term = p_v[r, i:i + 1, at] * ap_s[r, 0:order, :]
                total = term if total is None else total + term
            d_s[i, 0:order, at] = total
    deep = d_s.shape[1]
    high, low = halves(d_s[...].reshape(order * deep, cells))
    diagonal = (dot_nt(high, m_s[...]) + dot_nt(low, m_s[...])).reshape(order, deep, agg_count)
    wide = jnp.zeros((order, LANES - agg_count), F32)
    for i in range(order):
        for c in range(parts):
            line = jnp.concatenate([diagonal[i, firsts[c]:firsts[c] + counts[c], :], wide[0:counts[c]]], axis=1)
            op_s[pl.ds((op_row[c] + i * counts[c]) * 8, counts[c], stride=8), :] = line
    inverse = jnp.stack([op_s[pl.ds((op_row[c] + l) * 8, order, stride=counts[c] * 8), :][:, 0:agg_count]
                         for c in range(parts) for l in range(counts[c])])
    entry = lax.broadcasted_iota(jnp.int32, (order, agg_count), 0)
    row_at = lax.broadcasted_iota(jnp.int32, (order, 1, agg_count), 0)
    for pivot in range(order):
        line = inverse[pivot]
        scale = 1.0 / line[pivot:pivot + 1, :]
        line = jnp.where(entry == pivot, 1.0, line) * scale
        factor = inverse[:, pivot:pivot + 1, :]
        kept = jnp.where((entry == pivot)[None], 0.0, inverse)
        inverse = kept - factor * line[None]
        inverse = jnp.where(row_at == pivot, line[None], inverse)
    for i in range(order):
        small_s[16 * i + 32:16 * i + 32 + order, 0:agg_count] = inverse[i]

    loads[6].wait()
    z_s[...] = jnp.zeros_like(z_s)
    v_one[...] = jnp.zeros_like(v_one)

    def sweep():
        w_sent[1].wait_recv()
        split_vector(w_near)
        for k in range(rest):
            wacc_s[:, k * cells:(k + 1) * cells] += vector_part(oh_near, k)

        await_far(w_sent[0], w_far)
        split_vector(w_far)
        for k in range(rest):
            total = wacc_s[:, k * cells:(k + 1) * cells] + vector_part(oh_far, k)
            for t in range(tiles):
                wg_s[pl.ds(t * LANES + k + 1, 16, stride=8), :] = total[:, t * LANES:(t + 1) * LANES]

        for t in range(tiles):
            at = slice(t * LANES, (t + 1) * LANES)
            taken = [wg_s[t * LANES + j * 8:t * LANES + j * 8 + fine_rows, :] for j in range(order)]
            whole = None
            for r in range(order):
                total = None
                for j in range(order):
                    term = a_v[r, j, :, at] * taken[j]
                    total = term if total is None else total + term
                term = p_v[r, :, at] * jnp.sum(total, axis=0, keepdims=True)
                whole = term if whole is None else whole + term
            z_s[0:order, at] = whole

        high, low = halves(z_s[...])
        whl_s[0:16, :] = high
        whl_s[16:32, :] = low
        both = dot_nt(whl_s[...], m_s[...])
        residual = rhs_v[...] - (both[0:order, :] + both[16:16 + order, :])
        update = v_pad[0:order, :]
        for j in range(order):
            update = update + small_s[16 * j + 32:16 * j + 32 + order, 0:agg_count] * residual[j:j + 1, :]
        v_one[0:order, 0:agg_count] = update
        launch_far(v_sent)
        v_sent[1].start()

    def prepare():
        loads[5].wait()
        member = m_s[...]
        none = jnp.zeros_like(member)
        for k in range(rest):
            line = slot_v[k + 1:k + 2, :].astype(F32).astype(BF16)
            wide_line = jnp.broadcast_to(line, (agg_count, cells))
            for s in range(1, slots):
                picked = wide_line == jnp.full((agg_count, cells), s, BF16)
                rt_s[(s - 1) * agg_count:s * agg_count, k * cells:(k + 1) * cells] = jnp.where(picked, member, none)

        def q_tile(pair, t):

            lanes = pl.ds(pl.multiple_of(t * LANES, LANES), LANES)
            blocks = [[a_v[r, pair * 2 + jj, :, lanes] for r in range(order)] for jj in range(2)]
            for i in range(order):
                total = [None, None]
                for r in range(order):
                    basis = p_v[r, i:i + 1, lanes]
                    for jj in range(2):
                        term = basis * blocks[jj][r]
                        total[jj] = term if total[jj] is None else total[jj] + term
                for jj in range(2):
                    q_s[i, pair * 2 + jj, :, lanes] = total[jj]

        def q_step(step, carry):
            for half in range(2):
                q_tile(step // (tiles // 2), lax.rem(step, tiles // 2) * 2 + half)
            return carry

        lax.fori_loop(0, order // 2 * tiles // 2, q_step, 0)

        @pl.when(lazy)
        def meet_late():
            await_barrier()
            send_vector()
            send_basis(0)
            send_basis(1)

        @pl.when(bridges)
        def hand_on():
            w_up.wait_recv()
            pl.semaphore_wait(met_sem, 1)
            w_over.start()

        for c in range(parts):
            split_basis(pc_own, c)
            for k in range(rest):
                acc_s[at_row[c]:at_row[c] + tall[c], k * cells:(k + 1) * cells] = basis_part(oh_own, c, k)
        for c in range(parts):
            for copies in p_sent:
                copies[1].wait_recv()
            split_basis(pc_near, c)
            for k in range(rest):
                acc_s[at_row[c]:at_row[c] + tall[c], k * cells:(k + 1) * cells] += basis_part(oh_near, c, k)

        @pl.when(heads)
        def start_late():
            pl.semaphore_wait(met_sem, 1)
            for copies in p_sent:
                copies[0].start()

    def turn(at, carry):
        @pl.when(jnp.logical_xor(at == 0, tails))
        def run_prepare():
            prepare()

        @pl.when(at == 0)
        def run_sweep():
            sweep()

        return carry

    lax.fori_loop(0, 2, turn, 0)

    def product_part(c):
        pairs_here = counts[c] // 2

        def product_step(step, carry):
            for t in range(tiles):
                product_tile(step, t)
            return carry

        def product_tile(pair, t):
            lanes = pl.ds(pl.multiple_of(t * LANES, LANES), LANES)
            base = t * span + pair * 16
            taken = [[g_s[pl.ds(pl.multiple_of(base + (j * counts[c] + ll) * 8, 8), fine_rows), :]
                      for j in range(order)] for ll in range(2)]
            for i in range(order):
                total = [None, None]
                for j in range(order):
                    left = q_s[i, j, :, lanes]
                    for ll in range(2):
                        term = left * taken[ll][j]
                        total[ll] = term if total[ll] is None else total[ll] + term
                for ll in range(2):
                    prod_s[pl.ds(pl.multiple_of(base + (i * counts[c] + ll) * 8, 8), fine_rows), :] = total[ll]
        lax.fori_loop(0, pairs_here, product_step, 0)

    for c in range(parts):
        for copies, (a, b) in zip(p_sent, pieces):
            await_far(copies[0], pc_far.at[a:b])
        split_basis(pc_far, c)
        height = counts[c] * order
        for k in range(rest):
            total = acc_s[at_row[c]:at_row[c] + tall[c], k * cells:(k + 1) * cells] + basis_part(oh_far, c, k)
            for t in range(tiles):
                g_s[pl.ds(t * span + k + 1, height, stride=8), :] = total[0:height, t * LANES:(t + 1) * LANES]
        product_part(c)
        for k in range(rest):
            for t in range(tiles):
                high, low = halves(prod_s[pl.ds(t * span + k + 1, tall[c], stride=8), :])
                at = slice(k * cells + t * LANES, k * cells + (t + 1) * LANES)
                lhs_s[0:tall[c], at] = high
                lhs_s[tall[c]:2 * tall[c], at] = low
        both = dot_nt(lhs_s[0:2 * tall[c], :], rt_s[...])
        summed = both[0:height, :] + both[tall[c]:tall[c] + height, :]
        filler = jnp.zeros((height, LANES - agg_count), F32)
        for s in range(1, slots):
            part = summed[:, (s - 1) * agg_count:s * agg_count]
            op_s[pl.ds(op_row[c] * 8 + s, height, stride=8), :] = jnp.concatenate([part, filler], axis=1)

    v_sent[1].wait_recv()
    small_s[0:16, :] = jnp.concatenate([v_one[:, 0:agg_count], v_near[:, 0:agg_count]], axis=1)
    await_far(v_sent[0], v_far)
    small_s[16:32, :] = v_far[...]
    for copies in [v_sent] + p_sent:
        copies[1].wait_send()

        @pl.when(has_far)
        def drain():
            copies[0].wait_send()

    w_sent[1].wait_send()

    @pl.when(jnp.logical_and(has_far, jnp.logical_not(heads)))
    def drain_direct():
        w_sent[0].wait_send()

    @pl.when(heads)
    def drain_up():
        w_up.wait_send()

    @pl.when(bridges)
    def drain_over():
        w_over.wait_send()


def finish(n_fine, n_coarse, op_s, small_s, cc_v, rhs_v, op_ref, it_ref, cc_s):
    odd = lax.rem(lax.axis_index("coarse"), 2)
    is_odd = jnp.full((8, LANES), odd, jnp.int32)
    order, agg_count = rhs_v.shape
    slots = cc_v.shape[0]
    cc_s[...] = jnp.zeros_like(cc_s)
    cc_s[0:slots, 0:agg_count] = cc_v[...]
    column = cc_s[...]
    lane = jnp.bitwise_and(column, agg_count - 1)
    holder = column // agg_count
    is_near = holder == 2 - 2 * is_odd
    is_far = holder == 2 * is_odd
    first = lane + jnp.where(is_near, agg_count, 0)
    names = []
    for l in range(order):
        one_side = lane_gather(jnp.broadcast_to(small_s[l:l + 1, :], (8, LANES)), first)
        other = lane_gather(jnp.broadcast_to(small_s[16 + l:17 + l, :], (8, LANES)), lane)
        names.append(jnp.where(is_far, other, one_side)[0:slots, 0:agg_count])
    update = small_s[0:order, 0:agg_count]
    for i in range(order):
        total = None
        for l in range(order):
            row = (i * order + l) * 8
            block = op_s[row:row + slots, 0:agg_count]
            op_ref[i, l] = block
            term = block * names[l]
            total = term if total is None else total + term
        line = rhs_v[i:i + 1, :] - jnp.sum(total, axis=0, keepdims=True)
        update = update + small_s[16 * i + 32:16 * i + 32 + order, 0:agg_count] * line
    it_ref[...] = update


def body(n_fine, n_coarse, fine_blocks, fine_columns, coarse_slots, ghost_lists, tentative, members, coarse_columns,
         coarse_rhs, coarse_guess):
    fine_rows, order, _, cells = fine_blocks.shape
    slots, agg_count = coarse_columns.shape
    rest = fine_rows - 1
    ghosts = ghost_lists.reshape(-1, LANES)
    deep = -(-order * order // 16) * 16
    vm = pltpu.VMEM
    scratch = [
        vm((order, order, fine_rows, cells), F32), vm(fine_columns.shape, jnp.int32), vm(coarse_slots.shape, jnp.int32),
        vm(ghosts.shape, jnp.int32), vm(tentative.shape, F32), vm(members.shape, jnp.int32),
        vm(coarse_rhs.shape, F32), vm(coarse_guess.shape, F32),
        vm((16, agg_count), F32),
        vm((16, LANES), F32), vm((16, LANES), F32), vm((16, LANES), F32),
        vm((cells, agg_count), BF16), vm((agg_count, cells), BF16),
        vm((16, cells), F32), vm((16, cells), F32), vm((16, cells), F32), vm((16, cells), F32),
        vm((deep, cells), F32), vm((deep, cells), F32), vm((deep, cells), F32),
        vm((order, order, fine_rows, cells), F32), vm((order, 16, LANES), F32), vm((order, 16, cells), F32),
        vm((4, 8, cells), jnp.int32),
        vm((cells, rest * cells), BF16), vm((cells, rest * cells), BF16), vm((cells, rest * cells), BF16),
        vm((deep, 2 * cells), BF16), vm((32, cells), BF16), vm((16, rest * cells), F32),
        vm((cells // LANES * LANES, LANES), F32),
        vm((deep, rest * cells), F32),
        vm((cells // LANES * deep * 8, LANES), F32), vm((cells // LANES * deep * 8, LANES), F32),
        vm((16, cells), F32), vm((2 * deep, rest * cells), BF16), vm(((slots - 1) * agg_count, rest * cells), BF16),
        pltpu.SemaphoreType.DMA((7 + order // 2,)), pltpu.SemaphoreType.DMA((10,)), pltpu.SemaphoreType.DMA((9,)),
        pltpu.SemaphoreType.REGULAR,
    ]
    in_vmem = pl.BlockSpec(memory_space=pltpu.VMEM)
    padded, small = pl.pallas_call(
        functools.partial(kernel, n_fine, n_coarse),
        out_shape=(vm((order * order * 8, LANES), F32), vm((16 * order + 32, LANES), F32)),
        in_specs=[pl.BlockSpec(memory_space=pltpu.HBM)] * 8,
        out_specs=[in_vmem] * 2,
        scratch_shapes=scratch,
        compiler_params=pltpu.CompilerParams(collective_id=0, has_side_effects=True, vmem_limit_bytes=40 * 2**20),
    )(*[pltpu.with_memory_space_constraint(given, pltpu.HBM) for given in (
        jnp.transpose(fine_blocks, (1, 2, 0, 3)), fine_columns, coarse_slots, ghosts, tentative, members, coarse_rhs,
        coarse_guess)])
    op, iterate = pl.pallas_call(
        functools.partial(finish, n_fine, n_coarse),
        out_shape=(jax.ShapeDtypeStruct((order, order, slots, agg_count), F32),
                   jax.ShapeDtypeStruct((order, agg_count), F32)),
        in_specs=[in_vmem] * 4,
        out_specs=[in_vmem] * 2,
        scratch_shapes=[vm((8, LANES), jnp.int32)],
        compiler_params=pltpu.CompilerParams(vmem_limit_bytes=8 * 2**20),
    )(padded, small, coarse_columns, coarse_rhs)
    return jnp.transpose(op, (2, 0, 1, 3)), iterate


def solution(mesh):
    both = ("fine", "coarse")
    placed = (
        P(None, None, None, both), P(None, both), P(None, both), P(both), P(None, None, both), P(None, both),
        P(None, both), P(None, both), P(None, both),
    )
    return jax.shard_map(
        functools.partial(body, mesh.shape["fine"], mesh.shape["coarse"]),
        mesh=mesh,
        in_specs=placed,
        out_specs=(P(None, None, None, both), P(None, both)),
        check_vma=False,
    )
```
